32 devices in a mesh: dp: 16 (over z, y, x), tp: 2 (over core).
Axes of the slice: x: 2, y: 2, z: 4, core: 2. Of those that a mesh axis runs over, the one named last changes fastest.
Arguments:
- tokens: bfloat16 [32768, 768], P('dp'), may hold values from -6 to 6
- segment_ids: int32 [64, 512], P('dp'), may hold values from 0 to 7, never falling along the last dimension, each value on 1 to 256 neighbouring positions
- cotangent: bfloat16 [32768, 768], P('dp'), may hold values from -6 to 6
- w_query: bfloat16 [768, 768], P('dp', 'tp'), may hold values from -0.21875 to 0.21875
- w_key: bfloat16 [768, 768], P('dp', 'tp'), may hold values from -0.21875 to 0.21875
- w_value: bfloat16 [768, 768], P('dp', 'tp'), may hold values from -0.21875 to 0.21875
- w_output: bfloat16 [768, 768], P('tp', 'dp'), may hold values from -1.75 to 1.75
- shared_down: bfloat16 [768, 1024], P('dp'), may hold values from -0.21875 to 0.21875
- shared_up: bfloat16 [1024, 768], P('dp', 'tp'), may hold values from -0.1875 to 0.1875
- w_in: bfloat16 [768, 3072], P('dp', 'tp'), may hold values from -0.21875 to 0.21875
- w_out: bfloat16 [3072, 768], P('tp', 'dp'), may hold values from -0.109375 to 0.109375
- gain_one: float32 [768], replicated, may hold values from 0.25 to 1.75
- gain_two: float32 [768], replicated, may hold values from 0.25 to 1.75
- query_scale: float32 [1024], replicated, may hold values from 0.25 to 1.25
- query_bias: float32 [768], replicated, may hold values from -1 to 1
- value_scale: float32 [1024], replicated, may hold values from 0.25 to 1.25
- value_bias: float32 [768], replicated, may hold values from -1 to 1
Outputs:
- output: bfloat16 [32768, 768], P(('dp', 'tp'))
- token_grad: float32 [32768, 768], P(('dp', 'tp'))
- query_scale_grad: float32 [1024], replicated
- query_bias_grad: float32 [768], replicated
- value_scale_grad: float32 [1024], replicated
- value_bias_grad: float32 [768], replicated
The draws below stay inside these ranges and needn't reach their ends.
Inputs may be any that keep to these rules, and one draw needn't show every extreme that they name: `segment_ids`: within each sequence of 512 tokens the ids never fall; one sentence spans 1 to 256 tokens, and some sentence spans exactly 256.
All inputs are finite; a program needn't handle non-finite values.
Results may differ from the reference program's by a relative error of at most 0.018.
Values may be sent and summed in bfloat16 or wider, within the bound.
A program may use at most 192 MiB of HBM per device.

```python
import math
import jax
import jax.numpy as jnp
import numpy as np
from jax import lax

D = 768
HEADS = 12
HD = 64
FF = 3072
RANK = 1024
SEQ_LEN = 512
SEQ_DEV = 4
TOK_DEV = 2048
SEQS = 64
TOKENS = 32768
N_DP = 16


def block_scale(own_key, dims, shards, low, top_value):
    def one(position, shards_of):
        steps = jax.random.uniform(jax.random.fold_in(jax.random.fold_in(own_key, 6), position), (shards_of,), jnp.float32, low / len(shards), top_value / len(shards))
        return jnp.repeat(jnp.exp(steps), dims[position] // shards_of).reshape((-1,) + (1,) * (len(dims) - position - 1))

    level = one(*shards[0])
    for cut in shards[1:]:
        level = level * one(*cut)
    return level


def profile(amount, total, reach, skew):
    portions = [(1 << 20) // math.isqrt(standing ** skew) + 1 for standing in range(2, amount + 1)]
    spare, given = total - reach - (amount - 1), [1] * (amount - 1)
    while spare > 0:
        free = [i for i in range(amount - 1) if given[i] < reach]
        whole, budget = sum([portions[i] for i in free]), spare
        for i in free:
            addition = min(reach - given[i], max(1, budget * portions[i] // whole), spare)
            given[i] = given[i] + addition
            spare = spare - addition
    return np.array([reach] + given)


def uneven(stream_key, amount, total, bound, lean):
    if amount == 2:
        one = jax.random.randint(stream_key, (), max(1, total - bound), min(bound, total - 1) + 1)
        return jnp.stack([one, total - one])
    sizes = jnp.asarray(profile(amount, total, bound, lean), jnp.int32)
    twos = (amount - 1) // 2
    giver, taker = sizes[1:1 + 2 * twos:2], sizes[2:2 + 2 * twos:2]
    room = jnp.minimum(giver - 1, bound - taker)
    shifted = jax.random.randint(jax.random.fold_in(stream_key, 1), (twos,), 0, 1 << 20) % (room + 1)
    sizes = sizes.at[1:1 + 2 * twos:2].set(giver - shifted).at[2:2 + 2 * twos:2].set(taker + shifted)
    return sizes[jax.random.permutation(jax.random.fold_in(stream_key, 2), amount)]


def noise(own_key, dims, scale, bound, cuts=(), kind=jnp.bfloat16):
    drawn = scale * jax.random.normal(own_key, dims, jnp.float32)
    if cuts:
        drawn = drawn * block_scale(own_key, dims, cuts, -0.22, 0.18)
    return jnp.clip(drawn, -bound, bound).astype(kind)


def setup_inputs(seed: int = 0) -> dict:
    key_of = jax.random.split(jax.random.key(seed), 18)
    return {
        "tokens": noise(key_of[0], (TOKENS, D), 1.0, 6.0, ((0, 16),)),
        "segment_ids": jax.vmap(lambda own: jnp.searchsorted(jnp.cumsum(uneven(own, max(4, SEQ_LEN // 64), SEQ_LEN, SEQ_LEN // 2, 1)), jnp.arange(SEQ_LEN), side="right"))(jax.random.split(key_of[1], SEQS)).reshape((SEQS, SEQ_LEN)).astype(jnp.int32),
        "cotangent": noise(key_of[2], (TOKENS, D), 1.0, 6.0, ((0, 16),)),
        "w_query": noise(key_of[3], (D, D), D ** -0.5, 0.21875, ((0, 16), (1, 2))),
        "w_key": noise(key_of[4], (D, D), D ** -0.5, 0.21875, ((0, 16), (1, 2))),
        "w_value": noise(key_of[5], (D, D), D ** -0.5, 0.21875, ((0, 16), (1, 2))),
        "w_output": noise(key_of[6], (D, D), (D // 64) ** -0.5, 1.75, ((0, 2), (1, 16))),
        "shared_down": noise(key_of[7], (D, RANK), D ** -0.5, 0.21875, ((0, 16),)),
        "shared_up": noise(key_of[8], (RANK, D), RANK ** -0.5, 0.1875, ((0, 16), (1, 2))),
        "w_in": noise(key_of[9], (D, FF), D ** -0.5, 0.21875, ((0, 16), (1, 2))),
        "w_out": noise(key_of[10], (FF, D), FF ** -0.5, 0.109375, ((0, 2), (1, 16))),
        "gain_one": jnp.clip(1.0 + 0.15 * jax.random.normal(key_of[11], (D,), jnp.float32), 0.25, 1.75),
        "gain_two": jnp.clip(1.0 + 0.15 * jax.random.normal(key_of[12], (D,), jnp.float32), 0.25, 1.75),
        "query_scale": jnp.clip(jax.random.uniform(key_of[13], (RANK,), jnp.float32, 0.25, 1.25), 0.25, 1.25),
        "query_bias": jnp.clip(jax.random.uniform(key_of[14], (D,), jnp.float32, -1.0, 1.0), -1.0, 1.0),
        "value_scale": jnp.clip(jax.random.uniform(key_of[15], (RANK,), jnp.float32, 0.25, 1.25), 0.25, 1.25),
        "value_bias": jnp.clip(jax.random.uniform(key_of[16], (D,), jnp.float32, -1.0, 1.0), -1.0, 1.0),
    }


@jax.custom_vjp
def low(v):
    return lax.optimization_barrier(v.astype(jnp.bfloat16)).astype(jnp.float32)

@jax.custom_vjp
def low_back(v):
    return v

def low_keep(v):
    return (low(v), None)

def low_pass(kept, grad):
    return (grad,)

def back_keep(v):
    return (v, None)

def back_low(kept, grad):
    return (low(grad),)
low.defvjp(low_keep, low_pass)
low_back.defvjp(back_keep, back_low)

def matmul(left, right):
    return jnp.dot(left, right, precision=lax.Precision.HIGHEST)

def layer_norm(values, gain):
    average = lax.optimization_barrier(jnp.mean(values, axis=-1, keepdims=True))
    centered = values - average
    variance = lax.optimization_barrier(jnp.mean(centered * centered, axis=-1, keepdims=True))
    return centered * lax.rsqrt(variance + 1e-05) * gain

def attend_sequence(parts):
    queries, keys, values, segments = parts
    raw = jnp.einsum('qhe,khe->hqk', queries, keys, precision=lax.Precision.HIGHEST) * (1.0 / math.sqrt(HD))
    same = segments[:, None] == segments[None, :]
    scores = low_back(jnp.where(same[None, :, :], raw, -1000000000.0))
    probs = jax.nn.softmax(scores, axis=-1)
    mixed = jnp.einsum('hqk,khe->qhe', low(probs), values, precision=lax.Precision.HIGHEST)
    return low(low_back(mixed))

def forward(tokens, segments, query_scale, query_bias, value_scale, value_bias, frozen):
    w_query, w_key, w_value, w_output, shared_down, shared_up, w_in, w_out, gain_one, gain_two = frozen
    projected = low_back(matmul(tokens, shared_down))
    query_delta = low_back(matmul(low(projected * query_scale), shared_up))
    value_delta = low_back(matmul(low(projected * value_scale), shared_up))
    queries = low(low_back(matmul(tokens, w_query) + query_bias * query_delta))
    keys = low(low_back(matmul(tokens, w_key)))
    values = low(low_back(matmul(tokens, w_value) + value_bias * value_delta))
    split = (SEQ_DEV, SEQ_LEN, HEADS, HD)
    mixed = lax.map(jax.checkpoint(attend_sequence), (queries.reshape(split), keys.reshape(split), values.reshape(split), segments))
    mixed = mixed.reshape(TOK_DEV, D)
    attention = low_back(matmul(mixed, w_output))
    hidden = layer_norm(tokens + attention, gain_one)
    activation = low_back(matmul(low(hidden), w_in))
    inner = low(jax.nn.gelu(activation, approximate=False))
    branch = low_back(matmul(inner, w_out))
    return layer_norm(hidden + branch, gain_two)

def reference(tokens, segment_ids, cotangent, w_query, w_key, w_value, w_output, shared_down, shared_up, w_in, w_out, gain_one, gain_two, query_scale, query_bias, value_scale, value_bias):
    frozen = tuple((matrix.astype(jnp.float32) for matrix in (w_query, w_key, w_value, w_output, shared_down, shared_up, w_in, w_out, gain_one, gain_two)))
    token_groups = tokens.astype(jnp.float32).reshape(N_DP, TOK_DEV, D)
    cotangent_groups = cotangent.astype(jnp.float32).reshape(N_DP, TOK_DEV, D)
    segment_groups = segment_ids.reshape(N_DP, SEQ_DEV, SEQ_LEN)
    adapters = (query_scale.astype(jnp.float32), query_bias.astype(jnp.float32), value_scale.astype(jnp.float32), value_bias.astype(jnp.float32))

    def one_group(totals, parts):
        group_tokens, group_segments, group_cotangent = parts

        def run(inputs, scale_q, bias_q, scale_v, bias_v):
            return forward(inputs, group_segments, scale_q, bias_q, scale_v, bias_v, frozen)
        result, pullback = jax.vjp(run, group_tokens, *adapters)
        gradients = pullback(group_cotangent)
        totals = tuple((total + grad for total, grad in zip(totals, gradients[1:])))
        return (totals, (result.astype(jnp.bfloat16), gradients[0]))
    start = (jnp.zeros((RANK,), jnp.float32), jnp.zeros((D,), jnp.float32), jnp.zeros((RANK,), jnp.float32), jnp.zeros((D,), jnp.float32))
    totals, (outputs, token_grads) = lax.scan(one_group, start, (token_groups, segment_groups, cotangent_groups))
    return (outputs.reshape(TOKENS, D), token_grads.reshape(TOKENS, D), totals[0], totals[1], totals[2], totals[3])
```

```python
import functools
import math

import jax
import jax.numpy as jnp
from jax import lax
from jax.experimental import pallas as pl
from jax.experimental.pallas import tpu as pltpu
from jax.sharding import PartitionSpec as P

HD = 64
SEQ_LEN = 512
TILE_ROWS = 16
MESH = pl.DeviceIdType.MESH


def normalize(values):
    average = jnp.mean(values, axis=-1, keepdims=True)
    centered = values - average
    variance = jnp.mean(centered * centered, axis=-1, keepdims=True)
    inverse = lax.rsqrt(variance + 1e-05)
    return (centered * inverse, inverse)


def norm_back(upstream, normed, inverse, gain):
    scaled = upstream * gain
    first = jnp.mean(scaled, axis=-1, keepdims=True)
    second = jnp.mean(scaled * normed, axis=-1, keepdims=True)
    return inverse * (scaled - first - normed * second)


def times_transposed(left, right):
    return lax.dot_general(
        left, right, (((1,), (1,)), ((), ())), preferred_element_type=jnp.float32
    )


def exact_gelu(values):
    return jax.nn.gelu(values, approximate=False)


def masked_scores(queries, keys, segments):
    raw = jnp.einsum("qhe,khe->hqk", queries, keys, preferred_element_type=jnp.float32) * (
        1.0 / math.sqrt(HD)
    )
    same = segments[:, None] == segments[None, :]
    return jnp.where(same[None, :, :], raw, -1000000000.0)


def attend_forward(parts):
    queries, keys, values, segments = parts
    scores = masked_scores(queries, keys, segments)
    top = jnp.max(scores, axis=-1, keepdims=True)
    powers = jnp.exp(scores - top)
    total = jnp.sum(powers, axis=-1, keepdims=True)
    weights_low = (powers / total).astype(jnp.bfloat16)
    mixed = jnp.einsum(
        "hqk,khe->qhe", weights_low, values, preferred_element_type=jnp.float32
    ).astype(jnp.bfloat16)
    return (mixed, (top + jnp.log(total))[:, :, 0])


def attend_backward(parts):
    queries, keys, values, segments, logsum, mixed_grad = parts
    scores = masked_scores(queries, keys, segments)
    probs = jnp.exp(scores - logsum[:, :, None])
    weights_low = probs.astype(jnp.bfloat16)
    value_grad = jnp.einsum(
        "hqk,qhe->khe", weights_low, mixed_grad, preferred_element_type=jnp.float32
    ).astype(jnp.bfloat16)
    prob_grad = jnp.einsum("qhe,khe->hqk", mixed_grad, values, preferred_element_type=jnp.float32)
    score_grad = (probs * (prob_grad - jnp.sum(probs * prob_grad, axis=-1, keepdims=True))).astype(
        jnp.bfloat16
    )
    factor = 1.0 / math.sqrt(HD)
    query_grad = (
        jnp.einsum("hqk,khe->qhe", score_grad, keys, preferred_element_type=jnp.float32) * factor
    ).astype(jnp.bfloat16)
    key_grad = (
        jnp.einsum("hqk,qhe->khe", score_grad, queries, preferred_element_type=jnp.float32) * factor
    ).astype(jnp.bfloat16)
    return (query_grad, key_grad, value_grad)


def gather_kernel(slabs, stride, orders, widths, *refs):
    count = len(orders)
    sources, targets = refs[:count], refs[count : 2 * count]
    own_sems, send_sems, recv_sems = refs[2 * count :]
    bits = slabs.bit_length() - 1
    place, core = lax.axis_index("dp"), lax.axis_index("tp")
    me = place // stride
    index = [(me // (1 << b)) % 2 for b in range(bits)]

    def partner(b):
        here = index[b]
        return (place + (1 - 2 * here) * ((1 << b) * stride), core)

    sibling = (place, 1 - core)
    barrier = pltpu.get_barrier_semaphore()
    for b in range(bits):
        pl.semaphore_signal(barrier, inc=1, device_id=partner(b), device_id_type=MESH)
    pl.semaphore_signal(barrier, inc=1, device_id=sibling, device_id_type=MESH)
    pl.semaphore_wait(barrier, bits + 1)

    def view(target, done):
        where = tuple(slice(None) if b in done else index[b] for b in reversed(range(bits)))
        return target.at[(core,) + where]

    owns, copies = [], {}
    for i in range(count):
        source = sources[i]
        own = pltpu.make_async_copy(source, view(targets[i], ()), own_sems.at[i])
        own.start()
        owns.append(own)

    def start(i, step):
        if step == 0:
            source, target, device = sources[i], view(targets[i], ()), partner(orders[i][0])
        elif step < bits:
            source = target = view(targets[i], orders[i][:step])
            device = partner(orders[i][step])
        else:
            source = target = targets[i].at[core]
            device = sibling
        copy = pltpu.make_async_remote_copy(
            src_ref=source,
            dst_ref=target,
            send_sem=send_sems.at[i, step],
            recv_sem=recv_sems.at[i, step],
            device_id=device,
            device_id_type=MESH,
        )
        copy.start()
        copies[i, step] = copy

    ahead = 2
    for tick in range(count + (bits + 1) * ahead + 1):
        for step in range(bits + 1, -1, -1):
            i = tick - step * ahead
            if 0 <= i < count:
                if step > 0:
                    copies[i, step - 1].wait_recv()
                if step == 1:
                    owns[i].wait()
                if step <= bits:
                    start(i, step)
    for copy in copies.values():
        copy.wait_send()


def gather_weights(shards, orders, slabs, stride):
    bits = slabs.bit_length() - 1
    count = len(shards)
    shapes = [
        jax.ShapeDtypeStruct((2,) + (2,) * bits + s.shape, s.dtype) for s in shards
    ]
    full = pl.pallas_call(
        functools.partial(gather_kernel, slabs, stride, orders, None),
        out_shape=shapes,
        in_specs=[pl.BlockSpec(memory_space=pl.ANY)] * count,
        out_specs=[pl.BlockSpec(memory_space=pl.ANY)] * count,
        scratch_shapes=[
            pltpu.SemaphoreType.DMA((count,)),
            pltpu.SemaphoreType.DMA((count, bits + 1)),
            pltpu.SemaphoreType.DMA((count, bits + 1)),
        ],
        compiler_params=pltpu.CompilerParams(collective_id=0, has_side_effects=True),
        name="gather_weights",
    )(*shards)
    return [f.reshape((2, slabs * s.shape[0], s.shape[1])) for f, s in zip(full, shards)]


def beside(full):
    return jnp.concatenate([full[0], full[1]], axis=1)


def per_device(
    n_dp,
    tokens,
    segment_ids,
    cotangent,
    w_query,
    w_key,
    w_value,
    w_output,
    shared_down,
    shared_up,
    w_in,
    w_out,
    gain_one,
    gain_two,
    query_scale,
    query_bias,
    value_scale,
    value_bias,
):
    core = lax.axis_index("tp")
    rows = tokens.shape[0] // 2
    tokens = lax.dynamic_slice_in_dim(tokens, core * rows, rows, 0)
    cotangent = lax.dynamic_slice_in_dim(cotangent, core * rows, rows, 0)
    sequences = segment_ids.shape[0] // 2
    segment_ids = lax.dynamic_slice_in_dim(segment_ids, core * sequences, sequences, 0)

    down_half = shared_down.shape[1] // 2
    down_own = lax.dynamic_slice_in_dim(shared_down, core * down_half, down_half, 1)
    out_t = w_out.T
    quarter = w_in.shape[1] // 4
    shards = [w_query, w_key, w_value, w_output.T, down_own, shared_up]
    shards += [w_in[:, j * quarter : (j + 1) * quarter] for j in range(4)]
    shards += [out_t[:, j * quarter : (j + 1) * quarter] for j in range(4)]
    stride = 1
    while (w_query.shape[0] * stride) % TILE_ROWS or (shared_up.shape[0] * stride) % TILE_ROWS:
        stride *= 2
    if stride > 1:
        groups = [list(range(g * stride, (g + 1) * stride)) for g in range(n_dp // stride)]
        shards = [
            lax.all_gather(s, "dp", axis=0, tiled=True, axis_index_groups=groups) for s in shards
        ]
    slabs = n_dp // stride
    bits = slabs.bit_length() - 1
    far = list(range(bits - 1, -1, -1))
    first = tuple(far)
    second = tuple(far[:-2] + [0, 1])
    third = tuple([0, 1] + far[:-2])
    pick = {"A": first, "B": second, "C": third}
    orders = [pick[c] for c in "ABCABABCABABCA"]
    full = gather_weights(shards, orders, slabs, stride)
    query_full, key_full, value_full, output_t, down_full, up_full = [beside(f) for f in full[:6]]
    in_full = jnp.concatenate([full[6 + j][h] for h in range(2) for j in range(4)], axis=1)
    out_full_t = jnp.concatenate([full[10 + j][h] for h in range(2) for j in range(4)], axis=1)

    heads = query_full.shape[1] // HD
    projected = jnp.dot(tokens, down_full, preferred_element_type=jnp.float32)
    query_low = (projected * query_scale).astype(jnp.bfloat16)
    value_low = (projected * value_scale).astype(jnp.bfloat16)
    query_delta = jnp.dot(query_low, up_full, preferred_element_type=jnp.float32)
    value_delta = jnp.dot(value_low, up_full, preferred_element_type=jnp.float32)
    queries = (
        jnp.dot(tokens, query_full, preferred_element_type=jnp.float32) + query_bias * query_delta
    ).astype(jnp.bfloat16)
    keys = jnp.dot(tokens, key_full, preferred_element_type=jnp.float32).astype(jnp.bfloat16)
    values = (
        jnp.dot(tokens, value_full, preferred_element_type=jnp.float32) + value_bias * value_delta
    ).astype(jnp.bfloat16)
    split = (sequences, SEQ_LEN, heads, HD)
    query_blocks = queries.reshape(split)
    key_blocks = keys.reshape(split)
    value_blocks = values.reshape(split)
    mixed, logsum = lax.map(attend_forward, (query_blocks, key_blocks, value_blocks, segment_ids))
    mixed = mixed.reshape(rows, heads * HD)
    attention = times_transposed(mixed, output_t)
    normed_one, inverse_one = normalize(tokens.astype(jnp.float32) + attention)
    hidden = normed_one * gain_one
    hidden_low = hidden.astype(jnp.bfloat16)
    activation = jnp.dot(hidden_low, in_full, preferred_element_type=jnp.float32)
    inner, gelu_back = jax.vjp(exact_gelu, activation)
    branch = times_transposed(inner.astype(jnp.bfloat16), out_full_t)
    normed_two, inverse_two = normalize(hidden + branch)
    output = (normed_two * gain_two).astype(jnp.bfloat16)
    sum_two_grad = norm_back(cotangent.astype(jnp.float32), normed_two, inverse_two, gain_two)
    branch_grad = sum_two_grad.astype(jnp.bfloat16)
    inner_grad = jnp.dot(branch_grad, out_full_t, preferred_element_type=jnp.float32)
    (activation_grad,) = gelu_back(inner_grad)
    hidden_grad = sum_two_grad + times_transposed(activation_grad.astype(jnp.bfloat16), in_full)
    sum_one_grad = norm_back(hidden_grad, normed_one, inverse_one, gain_one)
    attention_grad = sum_one_grad.astype(jnp.bfloat16)
    mixed_grad = jnp.dot(attention_grad, output_t, preferred_element_type=jnp.float32).astype(
        jnp.bfloat16
    )
    query_grad, key_grad, value_grad = lax.map(
        attend_backward,
        (query_blocks, key_blocks, value_blocks, segment_ids, logsum, mixed_grad.reshape(split)),
    )
    query_grad = query_grad.reshape(rows, heads * HD)
    key_grad = key_grad.reshape(rows, heads * HD)
    value_grad = value_grad.reshape(rows, heads * HD)
    query_grad_wide = query_grad.astype(jnp.float32)
    value_grad_wide = value_grad.astype(jnp.float32)
    query_bias_part = jnp.sum(query_grad_wide * query_delta, axis=0)
    value_bias_part = jnp.sum(value_grad_wide * value_delta, axis=0)
    query_delta_grad = (query_grad_wide * query_bias).astype(jnp.bfloat16)
    value_delta_grad = (value_grad_wide * value_bias).astype(jnp.bfloat16)
    query_low_grad = times_transposed(query_delta_grad, up_full)
    value_low_grad = times_transposed(value_delta_grad, up_full)
    query_scale_part = jnp.sum(projected * query_low_grad, axis=0)
    value_scale_part = jnp.sum(projected * value_low_grad, axis=0)
    projected_grad = (query_low_grad * query_scale + value_low_grad * value_scale).astype(
        jnp.bfloat16
    )
    token_grad = (
        sum_one_grad
        + times_transposed(query_grad, query_full)
        + times_transposed(key_grad, key_full)
        + times_transposed(value_grad, value_full)
        + times_transposed(projected_grad, down_full)
    )
    sums = lax.psum(
        (query_scale_part, query_bias_part, value_scale_part, value_bias_part), ("dp", "tp")
    )
    return (output, token_grad) + sums


def solution(mesh):
    in_specs = (
        P("dp", None),
        P("dp", None),
        P("dp", None),
        P("dp", "tp"),
        P("dp", "tp"),
        P("dp", "tp"),
        P("tp", "dp"),
        P("dp", None),
        P("dp", "tp"),
        P("dp", "tp"),
        P("tp", "dp"),
        P(),
        P(),
        P(),
        P(),
        P(),
        P(),
    )
    out_specs = (P(("dp", "tp"), None), P(("dp", "tp"), None), P(), P(), P(), P())
    return jax.shard_map(
        functools.partial(per_device, mesh.shape["dp"]),
        mesh=mesh,
        in_specs=in_specs,
        out_specs=out_specs,
        check_vma=False,
    )
```

```python
import functools
import math
import types

import jax
import jax.numpy as jnp
from jax import lax
from jax.experimental import pallas as pl
from jax.experimental.pallas import tpu as pltpu
from jax.sharding import PartitionSpec as P

HD = 64
SEQ_LEN = 512
SPAN = SEQ_LEN // 2
LABELS = 8
LANES = 128
SLABS = 16
COPIES = 4
MASKED = -1000000000.0
MESH = pl.DeviceIdType.MESH
VMEM_LIMIT = 62 << 20


def dot(left, right):
    return jnp.dot(left, right, preferred_element_type=jnp.float32)


def dot_nt(left, right):
    return lax.dot_general(
        left, right, (((1,), (1,)), ((), ())), preferred_element_type=jnp.float32
    )


def dot_tn(left, right):
    return lax.dot_general(
        left, right, (((0,), (0,)), ((), ())), preferred_element_type=jnp.float32
    )


def normalize(values):
    average = jnp.mean(values, axis=-1, keepdims=True)
    centered = values - average
    variance = jnp.mean(centered * centered, axis=-1, keepdims=True)
    inverse = lax.rsqrt(variance + 1e-05)
    return centered * inverse, inverse


def norm_back(scaled, normed, inverse):
    first = jnp.mean(scaled, axis=-1, keepdims=True)
    second = jnp.mean(scaled * normed, axis=-1, keepdims=True)
    return inverse * (scaled - first - normed * second)


def gelu_and_slope(values):
    below = 0.5 * lax.erf(values * (1.0 / math.sqrt(2.0))) + 0.5
    bell = jnp.exp(values * values * -0.5) * (1.0 / math.sqrt(2.0 * math.pi))
    return values * below, below + values * bell


def own_lanes(pair):
    lane = lax.broadcasted_iota(jnp.int32, pair.shape, 1)
    zeros = jnp.zeros_like(pair)
    return jnp.concatenate([jnp.where(lane < HD, pair, zeros), jnp.where(lane < HD, zeros, pair)])


def join_heads(wide):
    n = wide.shape[1] // 2
    return jnp.concatenate([wide[:HD, :n], wide[HD:, n:]]).T


def label_rows(row):
    kind = lax.broadcasted_iota(jnp.int32, (LABELS, SEQ_LEN), 0)
    hot = jnp.where(kind == row, 1.0, 0.0)
    many = jnp.sum(hot, axis=1, keepdims=True)
    which = lax.broadcasted_iota(jnp.int32, (LABELS, 1), 0)
    first = jnp.min(jnp.where(many == float(SPAN), which, LABELS), axis=0, keepdims=True)
    start = jnp.sum(jnp.where(row < first, 1, 0), axis=1, keepdims=True)
    return hot, start


def roll_matrix(start, back):
    here = lax.broadcasted_iota(jnp.int32, (SEQ_LEN, SEQ_LEN), 1 if back else 0)
    there = lax.broadcasted_iota(jnp.int32, (SEQ_LEN, SEQ_LEN), 0 if back else 1)
    moved = here + start
    moved = jnp.where(moved >= SEQ_LEN, moved - SEQ_LEN, moved)
    return jnp.where(moved == there, 1.0, 0.0).astype(jnp.bfloat16)


PIECES = ((0, 0), (0, 1), (0, 3), (1, 0), (1, 0), (1, 1), (4, 1), (6, 0), (2, 0), (2, 2), (2, 1), (3, 0), (3, 0), (3, 2), (7, 1), (8, 2), (9, 0), (10, 1), (11, 0), (12, 1), (13, 3), (5, 1))
PLAN = (
    (0, (48, 24, 32, 8)),
    (1, (25, 40, 9, 0, 16, 41, 17, 112, 33, 1, 10, 56, 120, 49, 42, 26, 27, 34, 18, 57, 2, 11, 50, 19, 58, 3, 152, 153, 136, 35, 43, 113, 4, 121, 20, 51, 128, 59, 12)),
    (2, (64, 72, 73, 96, 80, 65, 88, 104, 97, 105, 89, 81, 66, 74, 160, 28, 114, 98, 129, 82, 90, 106, 144, 60, 75, 67, 83, 44, 91, 107, 99, 122, 130, 29, 36, 37, 45)),
    (3, (76, 68, 84, 115, 145, 154, 92, 161, 100, 137, 168, 52, 108, 69, 77, 85)),
    (4, (131, 93, 101, 109)),
    (0, {1: (146, 123), 2: (155,), 3: (162, 138)}),
    (-1, (116, 53)),
    (1, {1: (147,)}),
    (-1, (169, 139, 61)),
    (2, {1: (124,), 2: (156, 163, 132, 117), 4: (125,), 5: (148,), 6: (140, 170, 133)}),
    (-1, (141, 149, 157)),
    (3, {1: (164,)}),
    (5, ()),
    (-1, (171, 165)),
    (4, {}),
    (-1, (5, 13, 21)),
    (5, {2: (172,)}),
    (-1, (173,)),
    (6, {}),
)


def layer_kernel(stride, bits, groups, names, *refs):
    r = types.SimpleNamespace(**dict(zip(names, refs)))
    buffers = refs[len(names) :]
    place, core = lax.axis_index("dp"), lax.axis_index("tp")
    me = place // stride
    index = [(me // (1 << b)) % 2 for b in range(bits)]
    width = r.w_query.shape[1]
    rows, model = r.tok.shape
    quarters = r.win.shape[-1] // model
    seqs = rows // SEQ_LEN
    pairs = 2 * width // LANES
    bf16 = jnp.bfloat16

    def partner(b):
        return (place + (1 - 2 * index[b]) * ((1 << b) * stride), core)

    sibling = (place, 1 - core)

    far = list(range(bits - 1, -1, -1))
    near = far[:-2]
    orders = (tuple(far), tuple(near + [0, 1]), tuple([0, 1] + near), tuple([1, 0] + near))
    ranks = r.down.shape[1]
    half_rank = ranks // 2
    shards = [
        (r.up, r.up_full, width, 0),
        (r.w_key, r.key_full, width, 0),
        (r.query_own, r.query_full, width, 0),
        (r.value_own, r.value_full, width, 0),
        (r.out_t, r.out_full, width, 0),
        (r.down, r.down_full, half_rank, core * half_rank),
    ]
    shards += [(r.w_in, r.win, width, j * width) for j in range(quarters)]
    shards += [(r.ff_t, r.wout, width, j * width) for j in range(quarters)]
    seen, pieces = {}, []
    for name, order in PIECES:
        seen[name] = seen.get(name, 0) + 1
    taken = {}
    for name, order in PIECES:
        source, target, columns, offset = shards[name]
        part = columns // seen[name]
        at = taken.get(name, 0)
        taken[name] = at + 1
        first = offset + at * part
        if not isinstance(first, int):
            first = pl.multiple_of(first, LANES)
        wide = offset * 2 if isinstance(offset, int) else 0
        spot = pl.ds(pl.multiple_of(core * columns + wide + at * part, LANES), part)
        pieces.append((source.at[:, pl.ds(first, part)], target, spot, orders[order]))

    def view(i, done):
        where = tuple(slice(None) if b in done else index[b] for b in reversed(range(bits)))
        return pieces[i][1].at[where + (slice(None), pieces[i][2])]

    def own(i):
        return pltpu.make_async_copy(pieces[i][0], view(i, ()), r.own_sems.at[i])

    def remote(i, step):
        source, _, _, order = pieces[i]
        there = view(i, order[:step])
        return pltpu.make_async_remote_copy(
            src_ref=source if step == 0 else there,
            dst_ref=there,
            send_sem=r.send_sems.at[i, step],
            recv_sem=r.recv_sems.at[i, step],
            device_id=partner(order[step]) if step < bits else sibling,
            device_id_type=MESH,
        )

    def move(i, step):
        if step > 0:
            remote(i, step - 1).wait_recv()
        if step == 0:
            own(i).start()
        if step == 1:
            own(i).wait()
        if step <= bits:
            remote(i, step).start()

    def fetch(n, source, target):
        return pltpu.make_async_copy(source, target, r.in_sems.at[n])

    mine = pl.ds(pl.multiple_of(core * rows, rows), rows)
    get_tokens = fetch(0, r.tokens.at[mine], r.raw)
    get_cotangent = fetch(1, r.cotangent.at[mine], r.raw)

    def seq_rows(s):
        return pl.ds(pl.multiple_of(s * SEQ_LEN, SEQ_LEN), SEQ_LEN)

    def full(ref, first=0, count=None):
        value = ref[..., pl.ds(first, count or ref.shape[-1])]
        return value.reshape((value.shape[-2] * (1 << bits), value.shape[-1]))

    def prep():
        get_tokens.wait()
        every = r.segments[...]
        held = jnp.where(core == 0, every[:seqs], every[seqs:])
        found = []
        for s in range(seqs):
            hot, start = label_rows(held[s : s + 1])
            turn = roll_matrix(start, False)
            r.turn[s] = turn
            part = pl.ds(s * SEQ_LEN, SEQ_LEN)
            r.tok[part, :] = dot(turn, r.raw[part, :]).astype(bf16)
            turned = dot_nt(hot.astype(bf16), turn)[:, SPAN:]
            r.same[s] = dot_tn(turned, turned)
            found.append(jnp.where(start < SEQ_LEN, 0.0, MASKED))
        lowest = functools.reduce(jnp.minimum, found)
        r.lowest[...] = jnp.broadcast_to(lowest, r.lowest.shape)
        get_cotangent.start()

    def merge():
        columns = pl.ds(pl.multiple_of(core * width, width), width)
        up_half = r.up_full[..., columns]
        up_half = up_half.reshape((up_half.shape[-2] * (1 << bits), width))
        down = r.down[...].astype(jnp.float32)
        for scale, bias, weight, target in (
            (r.query_scale, r.query_bias, r.w_query, r.query_own),
            (r.value_scale, r.value_bias, r.w_value, r.value_own),
        ):
            scaled = (down * scale[...][None, :]).astype(bf16)
            extra = dot(scaled, up_half) * bias[columns][None, :]
            target[...] = (weight[...].astype(jnp.float32) + extra).astype(bf16)

    def project(weight, target, factor):
        def body(s, _):
            value = dot(r.tok[seq_rows(s), :], full(weight))
            target[seq_rows(s), :] = (value * factor).astype(bf16)
            return 0

        lax.fori_loop(0, seqs, body, 0)

    quads = [(s, half) for s in range(seqs) for half in range(2)]

    def masked(scores, s, half):
        if half == 0:
            return scores
        same = r.same[s] > 0.5
        return jnp.where(jnp.concatenate([same, same], axis=1), scores, MASKED)

    def attend(p):
        columns = pl.ds(pl.multiple_of(p * LANES, LANES), LANES)
        places = [pl.ds(s * SEQ_LEN + half * SPAN, SPAN) for s, half in quads]
        scores = [
            dot_nt(r.keys[here, columns], own_lanes(r.queries[here, columns])) for here in places
        ]
        powers, totals = [], []
        for n, (s, half) in enumerate(quads):
            score = masked(scores[n], s, half)
            top = jnp.max(score, axis=0, keepdims=True)
            power = jnp.exp(score - top)
            total = jnp.sum(power, axis=0, keepdims=True)
            r.logsum[n, pl.ds(p, 1), :] = top + jnp.log(total)
            r.lowest[n : n + 1, :] = jnp.minimum(r.lowest[n : n + 1, :], top)
            powers.append(power.astype(bf16))
            totals.append(total)
        for n, here in enumerate(places):
            mixed = dot(r.values[here, columns].T, powers[n]) * (1.0 / totals[n])
            r.mixed[here, columns] = join_heads(mixed).astype(bf16)

    def attend_back(p):
        columns = pl.ds(pl.multiple_of(p * LANES, LANES), LANES)
        places = [pl.ds(s * SEQ_LEN + half * SPAN, SPAN) for s, half in quads]
        queries = [own_lanes(r.queries[here, columns]) for here in places]
        grads = [own_lanes(r.mixed[here, columns]) for here in places]
        scores = [dot_nt(r.keys[here, columns], queries[n]) for n, here in enumerate(places)]
        firsts = [dot_nt(r.values[here, columns], grads[n]) for n, here in enumerate(places)]
        probs, lows = [], []
        for n, (s, half) in enumerate(quads):
            prob = jnp.exp(masked(scores[n], s, half) - r.logsum[n, pl.ds(p, 1), :])
            both = prob * firsts[n]
            total = jnp.sum(both, axis=0, keepdims=True)
            probs.append(prob.astype(bf16))
            lows.append((both - prob * total).astype(bf16))
        for n, here in enumerate(places):
            value_grad = dot(probs[n], grads[n])
            key_grad = dot(lows[n], queries[n])
            query_grad = join_heads(dot(r.keys[here, columns].T, lows[n]))
            for a, grad in enumerate((query_grad * (1.0 / math.sqrt(HD)), key_grad, value_grad)):
                spot = pl.ds(pl.multiple_of(a * model + p * LANES, LANES), LANES)
                r.inner[here, spot] = grad.astype(bf16)

    def first_norm(s):
        here = seq_rows(s)
        attention = dot_nt(r.mixed[here, :], full(r.out_full))
        normed, inverse = normalize(r.tok[here, :].astype(jnp.float32) + attention)
        r.normed[here, :] = normed
        r.inverse[here, :] = jnp.broadcast_to(inverse, (SEQ_LEN, LANES))
        r.hidden[here, :] = (normed * r.gain_one[...][None, :]).astype(bf16)

    def widen(it):
        j, s = it // seqs, it % seqs
        columns = pl.ds(pl.multiple_of(j * model, model), model)
        weight = r.win[..., columns]
        weight = weight.reshape((model, model))
        for n in range(SEQ_LEN // LANES):
            here = pl.ds(pl.multiple_of(s * SEQ_LEN + n * LANES, LANES), LANES)
            inner, slope = gelu_and_slope(dot(r.hidden[here, :], weight))
            r.inner[here, columns] = inner.astype(bf16)
            r.slope[here, columns] = slope.astype(bf16)

    most = (quarters - 1) * model

    def narrow(s):
        here = seq_rows(s)
        r.wide[here, :] = dot_nt(r.inner[here, :most], full(r.wout, 0, most))

    def second_norm(s):
        here = seq_rows(s)
        normed_one = r.normed[here, :]
        gain_one, gain_two = r.gain_one[...][None, :], r.gain_two[...][None, :]
        branch = r.wide[here, :] + dot_nt(r.inner[here, most:], full(r.wout, most, model))
        normed, inverse = normalize(normed_one * gain_one + branch)
        r.hidden[here, :] = (normed * gain_two).astype(bf16)
        turned = dot(r.turn[s], r.raw[here, :])
        grad = norm_back(turned * gain_two, normed, inverse)
        low = grad.astype(bf16)
        for j in range(quarters):
            inner_grad = dot(low, full(r.wout, j * model, model))
            slope = r.slope[here, pl.ds(j * model, model)].astype(jnp.float32)
            low_grad = (inner_grad * slope).astype(bf16)
            grad = grad + dot_nt(low_grad, full(r.win, j * model, model))
        back = norm_back(grad * gain_one, normed_one, r.inverse[here, :][:, :1])
        r.wide[here, :] = back
        r.mixed[here, :] = dot(back.astype(bf16), full(r.out_full)).astype(bf16)

    def rank(n):
        block = 2 * LANES
        columns = pl.ds(pl.multiple_of(n * block, block), block)
        eye = jnp.where(
            lax.broadcasted_iota(jnp.int32, (block, block), 0)
            == lax.broadcasted_iota(jnp.int32, (block, block), 1),
            1.0,
            0.0,
        ).astype(bf16)
        down = r.down_full[..., columns]
        down = down.reshape((down.shape[-2] * (1 << bits), block))
        down_t = dot_nt(eye, down).astype(bf16)
        r.projected[columns, :] = dot_nt(down_t, r.tok[...]).astype(bf16)

    def adapters(n):
        part = pl.ds(pl.multiple_of(n * 2 * LANES, 2 * LANES), 2 * LANES)
        low = r.projected[part, :]
        up = r.up_full[n // 2, n % 2].reshape((2 * LANES, model)).astype(jnp.float32)
        for a, first, scales, bias in (
            (0, 0, r.query_scale, r.query_bias),
            (2, 2 * model, r.value_scale, r.value_bias),
        ):
            product = dot(low, r.inner[:, first : first + model]) * up
            scale = jnp.broadcast_to(scales[part][None, :], (LANES, 2 * LANES)).T
            r.sums[a + 1 : a + 2, :model] += jnp.sum(product * scale[:, :1], axis=0, keepdims=True)
            over = jnp.sum(product * bias[...][None, :], axis=1, keepdims=True)
            r.sums[a : a + 1, part] = jnp.broadcast_to(over, (2 * LANES, LANES)).T[:1]

    def finish(s):
        here = seq_rows(s)
        grad = r.wide[here, :]
        for a, weight in enumerate((r.query_full, r.key_full, r.value_full)):
            grad = grad + dot_nt(r.inner[here, a * model : (a + 1) * model], full(weight))
        r.wide[here, :] = dot_tn(r.turn[s], grad.astype(bf16))

    def give(n, s, source, target):
        part = pl.ds(s * SEQ_LEN, SEQ_LEN)
        return pltpu.make_async_copy(source.at[part], target.at[part], r.out_sems.at[n, s])

    def peer(group, flip):
        there, other = place, core
        for n, bit in enumerate(group):
            if flip & (1 << n):
                if bit < 0:
                    other = 1 - core
                else:
                    there = there + (1 - 2 * ((place // (1 << bit)) % 2)) * (1 << bit)
        return (there, other)

    def spread(g):
        group, buffer = groups[g], buffers[g]
        digits = [core if bit < 0 else (place // (1 << bit)) % 2 for bit in group]
        mine = sum(digit * (1 << n) for n, digit in enumerate(digits))
        before = sum((1 << len(one)) - 1 for one in groups[:g])
        return [
            pltpu.make_async_remote_copy(
                src_ref=buffer.at[mine],
                dst_ref=buffer.at[mine],
                send_sem=r.total_sends.at[before + flip - 1],
                recv_sem=r.total_recvs.at[before + flip - 1],
                device_id=peer(group, flip),
                device_id_type=MESH,
            )
            for flip in range(1, 1 << len(group))
        ], mine

    def send_sums(g, value):
        copies, mine = spread(g)
        buffers[g][mine] = value
        for copy in copies:
            copy.start()

    def take_sums(g):
        for copy in spread(g)[0]:
            copy.wait_recv()
        value = buffers[g][0]
        for n in range(1, 1 << len(groups[g])):
            value = value + buffers[g][n]
        return value

    get_tokens.start()
    barrier = pltpu.get_barrier_semaphore()
    near_by = [partner(b) for b in range(bits)] + [sibling]
    near_by += [peer(g, flip) for g in groups for flip in range(1, 1 << len(g))]
    for device in near_by:
        pl.semaphore_signal(barrier, inc=1, device_id=device, device_id_type=MESH)
    pl.semaphore_wait(barrier, len(near_by))

    loops = (
        (pairs, attend),
        (seqs, first_norm),
        (quarters * seqs, widen),
        (seqs, narrow),
        (seqs, second_norm),
        (pairs, attend_back),
        (ranks // (2 * LANES), rank),
    )
    blocks = (
        prep,
        merge,
        lambda: project(r.key_full, r.keys, 1.0),
        lambda: project(r.query_full, r.queries, 1.0 / math.sqrt(HD)),
        lambda: project(r.value_full, r.values, 1.0),
        get_cotangent.wait,
    )

    def run_loop(count, body, inside):
        def step(it, _):
            for when, some in inside.items():

                @pl.when(it == when)
                def _(some=some):
                    for one in some:
                        move(one // 8, one % 8)

            body(it)
            return 0

        lax.fori_loop(0, count, step, 0)

    for block, moves in PLAN:
        if isinstance(moves, tuple):
            for one in moves:
                move(one // 8, one % 8)
            if block >= 0:
                blocks[block]()
        else:
            run_loop(*loops[block], moves)

    for s in range(seqs):
        here = seq_rows(s)
        r.raw[here, :] = dot_tn(r.turn[s], r.hidden[here, :]).astype(bf16)
        give(0, s, r.raw, r.o_output).start()
    r.sums[...] = jnp.zeros_like(r.sums)
    run_loop(ranks // (2 * LANES), adapters, {})
    lowest = jnp.min(jnp.min(r.lowest[...], axis=1, keepdims=True), axis=0, keepdims=True)
    r.sums[1:2, model : model + LANES] = jnp.broadcast_to(
        jnp.where(lowest > 0.5 * MASKED, 0.0, 1.0), (1, LANES)
    )
    for g in range(len(groups)):
        send_sums(g, r.sums[...] if g == 0 else total)
        if g < seqs:
            finish(g)
            give(1, g, r.wide, r.o_grad).start()
        total = take_sums(g)
    r.o_sums[...] = total
    r.o_flag[...] = total[1:2, model : model + 1]
    for i in range(len(pieces)):
        for step in range(bits + 1):
            remote(i, step).wait_send()
    for g in range(len(groups)):
        for copy in spread(g)[0]:
            copy.wait_send()
    for s in range(seqs):
        give(0, s, r.raw, r.o_output).wait()
        give(1, s, r.wide, r.o_grad).wait()


def hand_kernel(grad, output, sums, o_grad, o_output, *refs):
    held, sems = refs[4:6], refs[6]
    gets, puts = [], []
    for n, (source, middle, target) in enumerate(
        ((grad, held[0], o_grad), (output, held[1], o_output))
    ):
        rows = source.shape[0] // COPIES
        for c in range(COPIES):
            part = pl.ds(c * rows, rows)
            gets.append(pltpu.make_async_copy(source.at[part], middle.at[part], sems.at[0, n, c]))
            puts.append(pltpu.make_async_copy(middle.at[part], target.at[part], sems.at[1, n, c]))
    for get in gets:
        get.start()
    for n, out in enumerate(refs[:4]):
        out[...] = sums[n, : out.shape[0]]
    for get, put in zip(gets, puts):
        get.wait()
        put.start()
    for put in puts:
        put.wait()


def gather_kernel(slabs, stride, orders, *refs):
    count = len(orders)
    sources, targets = refs[:count], refs[count : 2 * count]
    own_sems, send_sems, recv_sems = refs[2 * count :]
    bits = slabs.bit_length() - 1
    place, core = lax.axis_index("dp"), lax.axis_index("tp")
    me = place // stride
    index = [(me // (1 << b)) % 2 for b in range(bits)]

    def partner(b):
        here = index[b]
        return (place + (1 - 2 * here) * ((1 << b) * stride), core)

    sibling = (place, 1 - core)
    barrier = pltpu.get_barrier_semaphore()
    for b in range(bits):
        pl.semaphore_signal(barrier, inc=1, device_id=partner(b), device_id_type=MESH)
    pl.semaphore_signal(barrier, inc=1, device_id=sibling, device_id_type=MESH)
    pl.semaphore_wait(barrier, bits + 1)

    def view(target, done):
        where = tuple(slice(None) if b in done else index[b] for b in reversed(range(bits)))
        return target.at[(core,) + where]

    owns, copies = [], {}
    for i in range(count):
        source = sources[i]
        own = pltpu.make_async_copy(source, view(targets[i], ()), own_sems.at[i])
        own.start()
        owns.append(own)

    def start(i, step):
        if step == 0:
            source, target, device = sources[i], view(targets[i], ()), partner(orders[i][0])
        elif step < bits:
            source = target = view(targets[i], orders[i][:step])
            device = partner(orders[i][step])
        else:
            source = target = targets[i].at[core]
            device = sibling
        copy = pltpu.make_async_remote_copy(
            src_ref=source,
            dst_ref=target,
            send_sem=send_sems.at[i, step],
            recv_sem=recv_sems.at[i, step],
            device_id=device,
            device_id_type=MESH,
        )
        copy.start()
        copies[i, step] = copy

    ahead = 2
    for tick in range(count + (bits + 1) * ahead + 1):
        for step in range(bits + 1, -1, -1):
            i = tick - step * ahead
            if 0 <= i < count:
                if step > 0:
                    copies[i, step - 1].wait_recv()
                if step == 1:
                    owns[i].wait()
                if step <= bits:
                    start(i, step)
    for copy in copies.values():
        copy.wait_send()


def gather_weights(shards, orders, slabs, stride):
    bits = slabs.bit_length() - 1
    count = len(shards)
    shapes = [
        jax.ShapeDtypeStruct((2,) + (2,) * bits + s.shape, s.dtype) for s in shards
    ]
    full = pl.pallas_call(
        functools.partial(gather_kernel, slabs, stride, orders),
        out_shape=shapes,
        in_specs=[pl.BlockSpec(memory_space=pl.ANY)] * count,
        out_specs=[pl.BlockSpec(memory_space=pl.ANY)] * count,
        scratch_shapes=[
            pltpu.SemaphoreType.DMA((count,)),
            pltpu.SemaphoreType.DMA((count, bits + 1)),
            pltpu.SemaphoreType.DMA((count, bits + 1)),
        ],
        compiler_params=pltpu.CompilerParams(collective_id=1, has_side_effects=True),
        name="gather_weights",
    )(*shards)
    return [f.reshape((2, slabs * s.shape[0], s.shape[1])) for f, s in zip(full, shards)]


def beside(full):
    return jnp.concatenate([full[0], full[1]], axis=1)


def total_kernel(groups, in_ref, out_ref, *refs):
    count = len(groups)
    buffers = refs[:count]
    sends, recvs = refs[count:]
    place, core = lax.axis_index("dp"), lax.axis_index("tp")

    def digit(bit):
        return core if bit < 0 else (place // (1 << bit)) % 2

    def peer(group, flip):
        there, other = place, core
        for n, bit in enumerate(group):
            if flip & (1 << n):
                if bit < 0:
                    other = 1 - core
                else:
                    there = there + (1 - 2 * digit(bit)) * (1 << bit)
        return (there, other)

    barrier = pltpu.get_barrier_semaphore()
    signals = 0
    for group in groups:
        for flip in range(1, 1 << len(group)):
            pl.semaphore_signal(
                barrier, inc=1, device_id=peer(group, flip), device_id_type=MESH
            )
            signals += 1
    pl.semaphore_wait(barrier, signals)

    value = in_ref[...]
    sem, started = 0, []
    for group, buffer in zip(groups, buffers):
        mine = sum(digit(bit) * (1 << n) for n, bit in enumerate(group))
        buffer[mine] = value
        copies = []
        for flip in range(1, 1 << len(group)):
            copy = pltpu.make_async_remote_copy(
                src_ref=buffer.at[mine],
                dst_ref=buffer.at[mine],
                send_sem=sends.at[sem],
                recv_sem=recvs.at[sem],
                device_id=peer(group, flip),
                device_id_type=MESH,
            )
            copy.start()
            copies.append(copy)
            sem += 1
        for copy in copies:
            copy.wait_recv()
        started += copies
        value = buffer[0]
        for n in range(1, 1 << len(group)):
            value = value + buffer[n]
    out_ref[...] = value
    for copy in started:
        copy.wait_send()


def call_total(sums, n_dp):
    bits = n_dp.bit_length() - 1
    groups = [(-1, 0, 1)] + [tuple(range(b, min(b + 2, bits))) for b in range(2, bits, 2)]
    peers = sum((1 << len(g)) - 1 for g in groups)
    return pl.pallas_call(
        functools.partial(total_kernel, groups),
        out_shape=jax.ShapeDtypeStruct(sums.shape, sums.dtype),
        in_specs=[pl.BlockSpec(memory_space=pltpu.VMEM)],
        out_specs=pl.BlockSpec(memory_space=pltpu.VMEM),
        scratch_shapes=[pltpu.VMEM((1 << len(g),) + sums.shape, jnp.float32) for g in groups]
        + [pltpu.SemaphoreType.DMA((peers,)), pltpu.SemaphoreType.DMA((peers,))],
        compiler_params=pltpu.CompilerParams(collective_id=2, has_side_effects=True),
        name="total",
    )(sums)


SCORES, MIX, MIX_BACK = "qhe,khe->hqk", "hqk,khe->qhe", "hqk,qhe->khe"


def masked_scores(queries, keys, segments):
    raw = jnp.einsum(SCORES, queries, keys, preferred_element_type=jnp.float32)
    same = segments[:, None] == segments[None, :]
    return jnp.where(same[None, :, :], raw, MASKED)


def attend_forward(parts):
    queries, keys, values, segments = parts
    scores = masked_scores(queries, keys, segments)
    top = jnp.max(scores, axis=-1, keepdims=True)
    powers = jnp.exp(scores - top)
    total = jnp.sum(powers, axis=-1, keepdims=True)
    weights_low = (powers / total).astype(jnp.bfloat16)
    mixed = jnp.einsum(MIX, weights_low, values, preferred_element_type=jnp.float32)
    return mixed.astype(jnp.bfloat16), (top + jnp.log(total))[:, :, 0]


def attend_backward(parts):
    queries, keys, values, segments, logsum, mixed_grad = parts
    bf16, f32 = jnp.bfloat16, jnp.float32
    scores = masked_scores(queries, keys, segments)
    probs = jnp.exp(scores - logsum[:, :, None])
    value_grad = jnp.einsum(MIX_BACK, probs.astype(bf16), mixed_grad, preferred_element_type=f32)
    prob_grad = jnp.einsum(SCORES, mixed_grad, values, preferred_element_type=f32)
    total = jnp.sum(probs * prob_grad, axis=-1, keepdims=True)
    score_grad = (probs * (prob_grad - total)).astype(bf16)
    query_grad = jnp.einsum(MIX, score_grad, keys, preferred_element_type=f32)
    key_grad = jnp.einsum(MIX_BACK, score_grad, queries, preferred_element_type=f32)
    query_grad = query_grad * (1.0 / math.sqrt(HD))
    return query_grad.astype(bf16), key_grad.astype(bf16), value_grad.astype(bf16)


def whole_sequences(a, w):
    bf16 = jnp.bfloat16
    tokens, segments = a.tokens, a.segments
    rows, model = tokens.shape
    queries = (dot(tokens, w.query) * (1.0 / math.sqrt(HD))).astype(bf16)
    keys = dot(tokens, w.key).astype(bf16)
    values = dot(tokens, w.value).astype(bf16)
    split = (segments.shape[0], SEQ_LEN, model // HD, HD)
    blocks = [x.reshape(split) for x in (queries, keys, values)] + [segments]
    mixed, logsum = lax.map(attend_forward, tuple(blocks))
    attention = dot_nt(mixed.reshape(rows, model), w.out_t)
    normed_one, inverse_one = normalize(tokens.astype(jnp.float32) + attention)
    hidden = normed_one * a.gain_one
    branch, slopes = 0.0, []
    for w_in, ff_t in ((w.w_in, w.ff_t),):
        inner, back = jax.vjp(
            lambda x: jax.nn.gelu(x, approximate=False), dot(hidden.astype(bf16), w_in)
        )
        slopes.append(back)
        branch = branch + dot_nt(inner.astype(bf16), ff_t)
    normed_two, inverse_two = normalize(hidden + branch)
    output = (normed_two * a.gain_two).astype(bf16)
    grad = norm_back(a.cotangent.astype(jnp.float32) * a.gain_two, normed_two, inverse_two)
    low = grad.astype(bf16)
    for w_in, ff_t, back in ((w.w_in, w.ff_t, slopes[0]),):
        grad = grad + dot_nt(back(dot(low, ff_t))[0].astype(bf16), w_in)
    sum_one = norm_back(grad * a.gain_one, normed_one, inverse_one)
    mixed_grad = dot(sum_one.astype(bf16), w.out_t).astype(bf16)
    grads = lax.map(attend_backward, tuple(blocks) + (logsum, mixed_grad.reshape(split)))
    query_grad, key_grad, value_grad = [g.reshape(rows, model) for g in grads]
    token_grad = sum_one + dot_nt(query_grad, w.query) + dot_nt(key_grad, w.key)
    token_grad = token_grad + dot_nt(value_grad, w.value)
    low = dot(tokens, w.down).astype(bf16)
    sums = []
    for scale, bias, grad in (
        (a.query_scale, a.query_bias, query_grad),
        (a.value_scale, a.value_bias, value_grad),
    ):
        product = dot_tn(low, grad) * w.up.astype(jnp.float32)
        sums.append(jnp.sum(product * bias, axis=1))
        over = jnp.sum(product * scale[:, None], axis=0)
        sums.append(jnp.pad(over, (0, low.shape[1] - model)))
    return output, token_grad, jnp.stack(sums)


def call_layer(stride, bits, n_dp, a, rows):
    model = a.tokens.shape[1]
    slab, width = a.w_query.shape
    quarters = a.w_in.shape[1] // width
    ranks = a.down.shape[1]
    seqs, pairs = rows // SEQ_LEN, model // LANES
    bf16, f32 = jnp.bfloat16, jnp.float32
    lead = (2,) * bits
    square = lead + (slab, model)
    up_shape = lead + (a.up.shape[0], model)
    all_bits = n_dp.bit_length() - 1
    groups = [(-1, 0, 1)] + [tuple(range(b, min(b + 2, all_bits))) for b in range(2, all_bits, 2)]
    peers = sum((1 << len(g)) - 1 for g in groups)

    hbm = dict(
        tokens=a.tokens,
        cotangent=a.cotangent,
        w_key=a.w_key,
        out_t=a.out_t,
        w_in=a.w_in,
        ff_t=a.ff_t,
        up=a.up,
    )
    vmem = dict(
        segments=a.segments,
        w_query=a.w_query,
        w_value=a.w_value,
        down=a.down,
        gain_one=a.gain_one,
        gain_two=a.gain_two,
        query_scale=a.query_scale,
        query_bias=a.query_bias,
        value_scale=a.value_scale,
        value_bias=a.value_bias,
    )
    outs = dict(o_output=((rows, model), bf16), o_grad=((rows, model), f32))
    kept = dict(o_sums=((4, ranks), f32), o_flag=((1, 1), f32))
    scratch = dict(
        up_full=(up_shape, bf16),
        query_full=(square, bf16),
        key_full=(square, bf16),
        value_full=(square, bf16),
        out_full=(square, bf16),
        down_full=(lead + (slab, ranks), bf16),
        win=(lead + (slab, quarters * model), bf16),
        wout=(lead + (slab, quarters * model), bf16),
        query_own=((slab, width), bf16),
        value_own=((slab, width), bf16),
        raw=((rows, model), bf16),
        tok=((rows, model), bf16),
        turn=((seqs, SEQ_LEN, SEQ_LEN), bf16),
        same=((seqs, SPAN, SPAN), f32),
        lowest=((8, 2 * SPAN), f32),
        logsum=((2 * seqs, 8, 2 * SPAN), f32),
        queries=((rows, model), bf16),
        keys=((rows, model), bf16),
        values=((rows, model), bf16),
        mixed=((rows, model), bf16),
        normed=((rows, model), f32),
        inverse=((rows, LANES), f32),
        hidden=((rows, model), bf16),
        inner=((rows, quarters * model), bf16),
        slope=((rows, quarters * model), bf16),
        wide=((rows, model), f32),
        projected=((ranks, rows), bf16),
        sums=((4, ranks), f32),
    )
    sems = dict(
        own_sems=(len(PIECES),),
        send_sems=(len(PIECES), bits + 1),
        recv_sems=(len(PIECES), bits + 1),
        total_sends=(peers,),
        total_recvs=(peers,),
        in_sems=(2,),
        out_sems=(2, seqs),
    )
    names = tuple(hbm) + tuple(vmem) + tuple(outs) + tuple(kept) + tuple(scratch) + tuple(sems)
    results = pl.pallas_call(
        functools.partial(layer_kernel, stride, bits, groups, names),
        out_shape=[jax.ShapeDtypeStruct(*v) for v in (outs | kept).values()],
        in_specs=[pl.BlockSpec(memory_space=pl.ANY)] * len(hbm)
        + [pl.BlockSpec(memory_space=pltpu.VMEM)] * len(vmem),
        out_specs=[pl.BlockSpec(memory_space=pl.ANY)] * len(outs)
        + [pl.BlockSpec(memory_space=pltpu.VMEM)] * len(kept),
        scratch_shapes=[pltpu.VMEM(*v) for v in scratch.values()]
        + [pltpu.SemaphoreType.DMA(v) for v in sems.values()]
        + [pltpu.VMEM((1 << len(g), 4, ranks), f32) for g in groups],
        compiler_params=pltpu.CompilerParams(
            collective_id=0, has_side_effects=True, vmem_limit_bytes=VMEM_LIMIT
        ),
        name="layer",
    )(*hbm.values(), *vmem.values())
    return results


def call_hand(output, grad, sums):
    f32 = jnp.float32
    ranks, (rows, model) = sums.shape[1], grad.shape
    grad, output, *totals = pl.pallas_call(
        hand_kernel,
        out_shape=[
            jax.ShapeDtypeStruct(grad.shape, grad.dtype),
            jax.ShapeDtypeStruct(output.shape, output.dtype),
            jax.ShapeDtypeStruct((ranks,), f32),
            jax.ShapeDtypeStruct((model,), f32),
            jax.ShapeDtypeStruct((ranks,), f32),
            jax.ShapeDtypeStruct((model,), f32),
        ],
        in_specs=[pl.BlockSpec(memory_space=pl.ANY)] * 2 + [pl.BlockSpec(memory_space=pltpu.VMEM)],
        out_specs=[pl.BlockSpec(memory_space=pl.ANY)] * 2
        + [pl.BlockSpec(memory_space=pltpu.VMEM)] * 4,
        scratch_shapes=[
            pltpu.VMEM(grad.shape, grad.dtype),
            pltpu.VMEM(output.shape, output.dtype),
            pltpu.SemaphoreType.DMA((2, 2, COPIES)),
        ],
        compiler_params=pltpu.CompilerParams(vmem_limit_bytes=VMEM_LIMIT),
        name="hand",
    )(grad, output, sums)
    return (output, grad) + tuple(totals)


def per_device(
    n_dp,
    tokens,
    segment_ids,
    cotangent,
    w_query,
    w_key,
    w_value,
    w_output,
    shared_down,
    shared_up,
    w_in,
    w_out,
    gain_one,
    gain_two,
    query_scale,
    query_bias,
    value_scale,
    value_bias,
):
    rows, model = tokens.shape[0] // 2, tokens.shape[1]
    ranks = shared_down.shape[1]
    shards = dict(
        w_query=w_query,
        w_key=w_key,
        w_value=w_value,
        out_t=w_output.T,
        down=shared_down,
        up=shared_up,
        w_in=w_in,
        ff_t=w_out.T,
    )
    stride = n_dp // SLABS
    if stride > 1:
        groups = [list(range(g * stride, (g + 1) * stride)) for g in range(SLABS)]
        gather = functools.partial(lax.all_gather, axis=0, tiled=True, axis_index_groups=groups)
        shards = {n: gather(s, "dp") for n, s in shards.items()}
    arrays = types.SimpleNamespace(
        **shards,
        tokens=tokens,
        cotangent=cotangent,
        segments=segment_ids,
        gain_one=gain_one,
        gain_two=gain_two,
        query_scale=query_scale,
        query_bias=query_bias,
        value_scale=value_scale,
        value_bias=value_bias,
    )
    bits = SLABS.bit_length() - 1
    output, grad, sums, flag = call_layer(stride, bits, n_dp, arrays, rows)
    def halves():
        return call_hand(output, grad, sums)

    def whole():
        core = lax.axis_index("tp")
        own = types.SimpleNamespace(**vars(arrays))
        own.tokens = lax.dynamic_slice_in_dim(tokens, core * rows, rows, 0)
        own.cotangent = lax.dynamic_slice_in_dim(cotangent, core * rows, rows, 0)
        count = segment_ids.shape[0] // 2
        own.segments = lax.dynamic_slice_in_dim(segment_ids, core * count, count, 0)
        half = lax.dynamic_slice_in_dim(arrays.down, core * (ranks // 2), ranks // 2, 1)
        names = ("query", "key", "value", "out_t", "up", "down", "w_in", "ff_t")
        mine = [arrays.w_query, arrays.w_key, arrays.w_value, arrays.out_t, arrays.up, half]
        mine += [arrays.w_in, arrays.ff_t]
        order = tuple(range(bits - 1, -1, -1))
        full = gather_weights(mine, [order] * len(mine), SLABS, stride)
        full = [jnp.concatenate([f[0], f[1]], axis=1) for f in full]
        weights = types.SimpleNamespace(**dict(zip(names, full)))
        for scale, bias, name in (
            (query_scale, query_bias, "query"),
            (value_scale, value_bias, "value"),
        ):
            extra = dot((weights.down * scale).astype(jnp.bfloat16), weights.up) * bias
            setattr(weights, name, (getattr(weights, name) + extra).astype(jnp.bfloat16))
        output, token_grad, parts = whole_sequences(own, weights)
        return call_hand(output, token_grad, call_total(parts, n_dp))

    return lax.cond(flag[0, 0] == 0.0, halves, whole)


def solution(mesh):
    in_specs = (
        P("dp", None),
        P("dp", None),
        P("dp", None),
        P("dp", "tp"),
        P("dp", "tp"),
        P("dp", "tp"),
        P("tp", "dp"),
        P("dp", None),
        P("dp", "tp"),
        P("dp", "tp"),
        P("tp", "dp"),
        P(),
        P(),
        P(),
        P(),
        P(),
        P(),
    )
    out_specs = (P(("dp", "tp"), None), P(("dp", "tp"), None), P(), P(), P(), P())
    return jax.shard_map(
        functools.partial(per_device, mesh.shape["dp"]),
        mesh=mesh,
        in_specs=in_specs,
        out_specs=out_specs,
        check_vma=False,
    )
```

```python
import functools
import math
import types

import jax
import jax.numpy as jnp
from jax import lax
from jax.experimental import pallas as pl
from jax.experimental.pallas import tpu as pltpu
from jax.sharding import PartitionSpec as P

HD = 64
SEQ_LEN = 512
SPAN = SEQ_LEN // 2
LABELS = 8
LANES = 128
SLABS = 16
COPIES = 4
MASKED = -1000000000.0
MESH = pl.DeviceIdType.MESH
VMEM_LIMIT = 62 << 20


def dot(left, right):
    return jnp.dot(left, right, preferred_element_type=jnp.float32)


def dot_nt(left, right):
    return lax.dot_general(
        left, right, (((1,), (1,)), ((), ())), preferred_element_type=jnp.float32
    )


def dot_tn(left, right):
    return lax.dot_general(
        left, right, (((0,), (0,)), ((), ())), preferred_element_type=jnp.float32
    )


def normalize(values):
    average = jnp.mean(values, axis=-1, keepdims=True)
    centered = values - average
    variance = jnp.mean(centered * centered, axis=-1, keepdims=True)
    inverse = lax.rsqrt(variance + 1e-05)
    return centered * inverse, inverse


def norm_back(scaled, normed, inverse):
    first = jnp.mean(scaled, axis=-1, keepdims=True)
    second = jnp.mean(scaled * normed, axis=-1, keepdims=True)
    return inverse * (scaled - first - normed * second)


def gelu_and_slope(values):
    below = 0.5 * lax.erf(values * (1.0 / math.sqrt(2.0))) + 0.5
    bell = jnp.exp(values * values * -0.5) * (1.0 / math.sqrt(2.0 * math.pi))
    return values * below, below + values * bell


def own_lanes(pair):
    lane = lax.broadcasted_iota(jnp.int32, pair.shape, 1)
    zeros = jnp.zeros_like(pair)
    return jnp.concatenate([jnp.where(lane < HD, pair, zeros), jnp.where(lane < HD, zeros, pair)])


def join_heads(wide):
    n = wide.shape[1] // 2
    return jnp.concatenate([wide[:HD, :n], wide[HD:, n:]]).T


def label_rows(row):
    kind = lax.broadcasted_iota(jnp.int32, (LABELS, SEQ_LEN), 0)
    hot = jnp.where(kind == row, 1.0, 0.0)
    many = jnp.sum(hot, axis=1, keepdims=True)
    which = lax.broadcasted_iota(jnp.int32, (LABELS, 1), 0)
    first = jnp.min(jnp.where(many == float(SPAN), which, LABELS), axis=0, keepdims=True)
    start = jnp.sum(jnp.where(row < first, 1, 0), axis=1, keepdims=True)
    return hot, start


def roll_matrix(start, back):
    here = lax.broadcasted_iota(jnp.int32, (SEQ_LEN, SEQ_LEN), 1 if back else 0)
    there = lax.broadcasted_iota(jnp.int32, (SEQ_LEN, SEQ_LEN), 0 if back else 1)
    moved = here + start
    moved = jnp.where(moved >= SEQ_LEN, moved - SEQ_LEN, moved)
    return jnp.where(moved == there, 1.0, 0.0).astype(jnp.bfloat16)


PIECES = ((0, 0), (0, 4), (0, 1), (1, 1), (1, 1), (1, 1), (2, 1), (2, 1), (2, 6), (3, 4), (3, 0), (3, 0), (4, 3), (6, 1), (7, 1), (8, 1), (9, 7), (10, 5), (11, 7), (12, 1), (13, 6), (5, 1))
PLAN = (
    (0, (24, 16, 0, 8, 40, 32, 25, 1, 112, 104, 9, 17)),
    (1, (10, 41, 26, 136, 33, 2, 144, 128, 18, 96, 11, 27, 3, 42, 34, 120, 19, 160, 43, 97, 145, 12, 129, 113, 137, 20, 35, 4)),
    (-1, (88, 48, 64, 80, 72, 56, 49, 65, 89, 81, 73, 57, 50, 66, 74, 58, 82, 90, 152, 121, 105, 114, 75, 36, 59, 91, 44, 98, 67, 83, 28, 29, 37, 45)),
    (7, {1: (51, 60, 153, 106, 76, 115, 68)}),
    (-1, (130, 122, 52, 53, 61, 69)),
    (8, {1: (168, 107, 92, 99, 161, 154, 138, 84)}),
    (-1, (77, 85, 93)),
    (9, {1: (123, 146)}),
    (0, {3: (116, 131), 4: (162,), 5: (100, 139)}),
    (-1, (108, 101)),
    (1, {1: (169, 147, 155)}),
    (-1, (109,)),
    (2, {3: (163, 124), 4: (132, 117), 8: (125,), 10: (140,), 11: (156,), 12: (133,), 13: (148, 170)}),
    (-1, (141, 149, 157)),
    (3, {3: (164,)}),
    (2, ()),
    (-1, (171, 165)),
    (4, {6: (172,)}),
    (-1, (5, 13, 21)),
    (5, {}),
    (-1, (173,)),
    (6, {}),
)


def layer_kernel(stride, bits, groups, names, *refs):
    r = types.SimpleNamespace(**dict(zip(names, refs)))
    buffers = refs[len(names) :]
    place, core = lax.axis_index("dp"), lax.axis_index("tp")
    me = place // stride
    index = [(me // (1 << b)) % 2 for b in range(bits)]
    width = r.w_query.shape[1]
    rows, model = r.tok.shape
    quarters = r.win.shape[-1] // model
    seqs = rows // SEQ_LEN
    pairs = 2 * width // LANES
    bf16 = jnp.bfloat16

    def partner(b):
        return (place + (1 - 2 * index[b]) * ((1 << b) * stride), core)

    sibling = (place, 1 - core)

    top, rest = [bits - 1], list(range(bits - 2, 1, -1))
    orders = (
        top + rest + [1, 0],
        top + rest + [0, 1],
        [0, 1] + top + rest,
        [1, 0] + top + rest,
        top + [0, 1] + rest,
        top + [1, 0] + rest,
        top + [0] + rest + [1],
        top + [1] + rest + [0],
    )
    ranks = r.down.shape[1]
    half_rank = ranks // 2
    shards = [
        (r.up, r.up_full, width, 0, 0),
        (r.w_key, r.qkv_full, width, 0, model),
        (r.query_own, r.qkv_full, width, 0, 0),
        (r.value_own, r.qkv_full, width, 0, 2 * model),
        (r.out_t, r.out_full, width, 0, 0),
        (r.down, r.down_full, half_rank, core * half_rank, 0),
    ]
    shards += [(r.w_in, r.win, width, j * width, j * model) for j in range(quarters)]
    shards += [(r.ff_t, r.wout, width, j * width, j * model) for j in range(quarters)]
    seen, pieces = {}, []
    for name, order in PIECES:
        seen[name] = seen.get(name, 0) + 1
    taken = {}
    for name, order in PIECES:
        source, target, columns, offset, base = shards[name]
        part = columns // seen[name]
        at = taken.get(name, 0)
        taken[name] = at + 1
        first = offset + at * part
        if not isinstance(first, int):
            first = pl.multiple_of(first, LANES)
        spot = pl.ds(pl.multiple_of(core * columns + base + at * part, LANES), part)
        pieces.append((source.at[:, pl.ds(first, part)], target, spot, orders[order]))

    def view(i, done):
        where = tuple(slice(None) if b in done else index[b] for b in reversed(range(bits)))
        return pieces[i][1].at[where + (slice(None), pieces[i][2])]

    def own(i):
        return pltpu.make_async_copy(pieces[i][0], view(i, ()), r.own_sems.at[i])

    def remote(i, step):
        source, _, _, order = pieces[i]
        there = view(i, order[:step])
        return pltpu.make_async_remote_copy(
            src_ref=source if step == 0 else there,
            dst_ref=there,
            send_sem=r.send_sems.at[i, step],
            recv_sem=r.recv_sems.at[i, step],
            device_id=partner(order[step]) if step < bits else sibling,
            device_id_type=MESH,
        )

    def move(i, step):
        if step > 0:
            remote(i, step - 1).wait_recv()
        if step == 0:
            own(i).start()
        if step == 1:
            own(i).wait()
        if step <= bits:
            remote(i, step).start()

    def fetch(n, source, target):
        return pltpu.make_async_copy(source, target, r.in_sems.at[n])

    mine = pl.ds(pl.multiple_of(core * rows, rows), rows)
    get_tokens = fetch(0, r.tokens.at[mine], r.raw)
    get_cotangent = fetch(1, r.cotangent.at[mine], r.raw)

    def seq_rows(s):
        return pl.ds(pl.multiple_of(s * SEQ_LEN, SEQ_LEN), SEQ_LEN)

    def full(ref, first=0, count=None):
        value = ref[..., pl.ds(first, count or ref.shape[-1])]
        return value.reshape((value.shape[-2] * (1 << bits), value.shape[-1]))

    def prep():
        get_tokens.wait()
        every = r.segments[...]
        held = jnp.where(core == 0, every[:seqs], every[seqs:])
        found = []
        for s in range(seqs):
            hot, start = label_rows(held[s : s + 1])
            turn = roll_matrix(start, False)
            r.turn[s] = turn
            part = pl.ds(s * SEQ_LEN, SEQ_LEN)
            r.tok[part, :] = dot(turn, r.raw[part, :]).astype(bf16)
            turned = dot_nt(hot.astype(bf16), turn)[:, SPAN:]
            r.same[s] = dot_tn(turned, turned)
            found.append(jnp.where(start < SEQ_LEN, 0.0, MASKED))
        lowest = functools.reduce(jnp.minimum, found)
        r.lowest[...] = jnp.broadcast_to(lowest, r.lowest.shape)
        get_cotangent.start()

    def merge():
        columns = pl.ds(pl.multiple_of(core * width, width), width)
        up_half = r.up_full[..., columns]
        up_half = up_half.reshape((up_half.shape[-2] * (1 << bits), width))
        down = r.down[...].astype(jnp.float32)
        for scale, bias, weight, target in (
            (r.query_scale, r.query_bias, r.w_query, r.query_own),
            (r.value_scale, r.value_bias, r.w_value, r.value_own),
        ):
            scaled = (down * scale[...][None, :]).astype(bf16)
            extra = dot(scaled, up_half) * bias[columns][None, :]
            target[...] = (weight[...].astype(jnp.float32) + extra).astype(bf16)

    def project(first, target, factor):
        def body(s, hook):
            hook(0)
            value = dot(r.tok[seq_rows(s), :], full(r.qkv_full, first, model))
            target[seq_rows(s), :] = (value * factor).astype(bf16)

        return body

    quads = [(s, half) for s in range(seqs) for half in range(2)]

    def masked(scores, s, half):
        if half == 0:
            return scores
        same = r.same[s] > 0.5
        return jnp.where(jnp.concatenate([same, same], axis=1), scores, MASKED)

    places = [pl.ds(s * SEQ_LEN + half * SPAN, SPAN) for s, half in quads]

    def attend(p, hook):
        hook(0)
        columns = pl.ds(pl.multiple_of(p * LANES, LANES), LANES)
        scores = [
            dot_nt(r.keys[here, columns], own_lanes(r.queries[here, columns])) for here in places
        ]
        for n, (s, half) in enumerate(quads):
            score = masked(scores[n], s, half)
            top = jnp.max(score, axis=0, keepdims=True)
            power = jnp.exp(score - top)
            total = jnp.sum(power, axis=0, keepdims=True)
            r.lowest[n : n + 1, :] = jnp.minimum(r.lowest[n : n + 1, :], top)
            r.probs[p, n] = (power * (1.0 / total)).astype(bf16)
        for n, here in enumerate(places):
            mixed = dot(r.values[here, columns].T, r.probs[p, n])
            r.mixed[here, columns] = join_heads(mixed).astype(bf16)

    def attend_back(_, hook):
        blocks = [(p, n) for p in range(pairs) for n in range(len(quads))]
        fronts, lows = {}, {}

        def front(p, n):
            columns = pl.ds(p * LANES, LANES)
            grads = own_lanes(r.mixed[places[n], columns])
            return grads, dot_nt(r.values[places[n], columns], grads)

        def middle(p, n):
            prob = r.probs[p, n].astype(jnp.float32)
            both = prob * fronts[p, n][1]
            total = jnp.sum(both, axis=0, keepdims=True)
            return (both - prob * total).astype(bf16)

        def back(p, n):
            columns = pl.ds(p * LANES, LANES)
            value_grad = dot(r.probs[p, n], fronts[p, n][0])
            key_grad = dot(lows[p, n], own_lanes(r.queries[places[n], columns]))
            query_grad = join_heads(dot(r.keys[places[n], columns].T, lows[p, n]))
            query_grad = query_grad * (1.0 / math.sqrt(HD))
            for a, grad in enumerate((query_grad, key_grad, value_grad)):
                r.inner[places[n], pl.ds(a * model + p * LANES, LANES)] = grad.astype(bf16)

        for at in range(len(blocks) + 2):
            if at % len(quads) == 0 and at < len(blocks):
                hook(at // len(quads))
            if at < len(blocks):
                fronts[blocks[at]] = front(*blocks[at])
            if 1 <= at <= len(blocks):
                lows[blocks[at - 1]] = middle(*blocks[at - 1])
            if at >= 2:
                back(*blocks[at - 2])

    def parts(s, count):
        size = SEQ_LEN // count
        return [
            pl.ds(pl.multiple_of(s * SEQ_LEN + n * size, size), size) for n in range(count)
        ]

    def first_norm(s, hook):
        for n, here in enumerate(parts(s, 2)):
            hook(n)
            attention = dot_nt(r.mixed[here, :], full(r.out_full))
            normed, inverse = normalize(r.tok[here, :].astype(jnp.float32) + attention)
            r.normed[here, :] = normed
            r.inverse[here, :] = jnp.broadcast_to(inverse, (inverse.shape[0], LANES))
            r.hidden[here, :] = (normed * r.gain_one[...][None, :]).astype(bf16)

    def widen(it, hook):
        j, s = it // seqs, it % seqs
        columns = pl.ds(pl.multiple_of(j * model, model), model)
        hook(0)
        weight = r.win[..., columns]
        weight = weight.reshape((model, model))
        for n, here in enumerate(parts(s, SEQ_LEN // LANES)):
            if n == SEQ_LEN // LANES // 2:
                hook(1)
            inner, slope = gelu_and_slope(dot(r.hidden[here, :], weight))
            r.inner[here, columns] = inner.astype(bf16)
            r.slope[here, columns] = slope.astype(bf16)

    most = (quarters - 1) * model

    def narrow(s, hook):
        for n, here in enumerate(parts(s, 2)):
            hook(n)
            r.wide[here, :] = dot_nt(r.inner[here, :most], full(r.wout, 0, most))

    def second_norm(s, hook):
        gain_one, gain_two = r.gain_one[...][None, :], r.gain_two[...][None, :]
        halves = parts(s, 2)
        grads, lows = [], []
        hook(0)
        for here in halves:
            branch = r.wide[here, :] + dot_nt(r.inner[here, most:], full(r.wout, most, model))
            normed, inverse = normalize(r.normed[here, :] * gain_one + branch)
            r.hidden[here, :] = (normed * gain_two).astype(bf16)
            grad = norm_back(r.raw[here, :].astype(jnp.float32) * gain_two, normed, inverse)
            grads.append(grad)
            lows.append(grad.astype(bf16))
        for j in range(quarters):
            if j:
                hook(j)
            part = pl.ds(j * model, model)
            inner = [
                dot(low, full(r.wout, j * model, model)) * r.slope[here, part].astype(jnp.float32)
                for low, here in zip(lows, halves)
            ]
            grads = [
                grad + dot_nt(one.astype(bf16), full(r.win, j * model, model))
                for grad, one in zip(grads, inner)
            ]
        for grad, here in zip(grads, halves):
            back = norm_back(grad * gain_one, r.normed[here, :], r.inverse[here, :][:, :1])
            r.wide[here, :] = back
            r.mixed[here, :] = dot(back.astype(bf16), full(r.out_full)).astype(bf16)

    def cotangents():
        get_cotangent.wait()
        for s in range(seqs):
            here = pl.ds(s * SEQ_LEN, SEQ_LEN)
            r.raw[here, :] = dot(r.turn[s], r.raw[here, :]).astype(bf16)

    def rank(s, hook):
        hook(0)
        here = seq_rows(s)
        r.slope[here, :ranks] = dot(r.tok[here, :], full(r.down_full)).astype(bf16)

    def adapters(n, hook):
        block = ranks // 2
        part = pl.ds(pl.multiple_of(n * block, block), block)
        low = r.slope[:, part]
        up = r.up_full[n].reshape((block, model)).astype(jnp.float32)
        kinds = ((0, 0, r.query_scale, r.query_bias), (2, 2 * model, r.value_scale, r.value_bias))
        products = [dot_tn(low, r.inner[:, first : first + model]) for _, first, _, _ in kinds]
        for product, (a, _, scales, bias) in zip(products, kinds):
            product = product * up
            scale = jnp.broadcast_to(scales[part][None, :], (LANES, block)).T
            r.sums[a + 1 : a + 2, :model] += jnp.sum(product * scale[:, :1], axis=0, keepdims=True)
            over = jnp.sum(product * bias[...][None, :], axis=1, keepdims=True)
            r.sums[a : a + 1, part] = jnp.broadcast_to(over, (block, LANES)).T[:1]

    def finish(s):
        here = seq_rows(s)
        grad = r.wide[here, :] + dot_nt(r.inner[here, : 3 * model], full(r.qkv_full))
        r.mixed[here, :] = dot_tn(r.turn[s], grad.astype(bf16)).astype(bf16)

    def give(n, s, source, target):
        part = pl.ds(s * SEQ_LEN, SEQ_LEN)
        return pltpu.make_async_copy(source.at[part], target.at[part], r.out_sems.at[n, s])

    def peer(group, flip):
        there, other = place, core
        for n, bit in enumerate(group):
            if flip & (1 << n):
                if bit < 0:
                    other = 1 - core
                else:
                    there = there + (1 - 2 * ((place // (1 << bit)) % 2)) * (1 << bit)
        return (there, other)

    def spread(g):
        group, buffer = groups[g], buffers[g]
        digits = [core if bit < 0 else (place // (1 << bit)) % 2 for bit in group]
        mine = sum(digit * (1 << n) for n, digit in enumerate(digits))
        before = sum((1 << len(one)) - 1 for one in groups[:g])
        return [
            pltpu.make_async_remote_copy(
                src_ref=buffer.at[mine],
                dst_ref=buffer.at[mine],
                send_sem=r.total_sends.at[before + flip - 1],
                recv_sem=r.total_recvs.at[before + flip - 1],
                device_id=peer(group, flip),
                device_id_type=MESH,
            )
            for flip in range(1, 1 << len(group))
        ], mine

    def send_sums(g, value):
        copies, mine = spread(g)
        buffers[g][mine] = value
        for copy in copies:
            copy.start()

    def take_sums(g):
        for copy in spread(g)[0]:
            copy.wait_recv()
        value = buffers[g][0]
        for n in range(1, 1 << len(groups[g])):
            value = value + buffers[g][n]
        return value

    get_tokens.start()
    barrier = pltpu.get_barrier_semaphore()
    near_by = [partner(b) for b in range(bits)] + [sibling]
    near_by += [peer(g, flip) for g in groups for flip in range(1, 1 << len(g))]
    for device in near_by:
        pl.semaphore_signal(barrier, inc=1, device_id=device, device_id_type=MESH)
    pl.semaphore_wait(barrier, len(near_by))

    loops = (
        (pairs, 1, attend),
        (seqs, 2, first_norm),
        (quarters * seqs, 2, widen),
        (seqs, 2, narrow),
        (seqs, quarters, second_norm),
        (1, pairs, attend_back),
        (seqs, 1, rank),
        (seqs, 1, project(model, r.keys, 1.0)),
        (seqs, 1, project(0, r.queries, 1.0 / math.sqrt(HD))),
        (seqs, 1, project(2 * model, r.values, 1.0)),
    )
    blocks = (prep, merge, cotangents)

    def run_loop(count, spots, body, inside):
        def step(it, _):
            def hook(spot):
                for when, some in inside.items():
                    if when % spots != spot:
                        continue

                    @pl.when(it == when // spots)
                    def _(some=some):
                        for one in some:
                            move(one // 8, one % 8)

            body(it, hook)
            return 0

        def once(spot):
            for one in inside.get(spot, ()):
                move(one // 8, one % 8)

        if count == 1:
            body(0, once)
        else:
            lax.fori_loop(0, count, step, 0)

    for block, moves in PLAN:
        if isinstance(moves, tuple):
            for one in moves:
                move(one // 8, one % 8)
            if block >= 0:
                blocks[block]()
        else:
            run_loop(*loops[block], moves)

    for s in range(seqs):
        here = seq_rows(s)
        r.raw[here, :] = dot_tn(r.turn[s], r.hidden[here, :]).astype(bf16)
        give(0, s, r.raw, r.o_output).start()
    r.sums[...] = jnp.zeros_like(r.sums)
    run_loop(2, 1, adapters, {})
    lowest = jnp.min(jnp.min(r.lowest[...], axis=1, keepdims=True), axis=0, keepdims=True)
    r.sums[1:2, model : model + LANES] = jnp.broadcast_to(
        jnp.where(lowest > 0.5 * MASKED, 0.0, 1.0), (1, LANES)
    )
    for g in range(len(groups)):
        send_sums(g, r.sums[...] if g == 0 else total)
        if g < seqs:
            finish(g)
            give(1, g, r.mixed, r.o_grad).start()
        total = take_sums(g)
    r.o_sums[...] = total
    r.o_flag[...] = total[1:2, model : model + 1]
    for i in range(len(pieces)):
        for step in range(bits + 1):
            remote(i, step).wait_send()
    for g in range(len(groups)):
        for copy in spread(g)[0]:
            copy.wait_send()
    for s in range(seqs):
        give(0, s, r.raw, r.o_output).wait()
        give(1, s, r.mixed, r.o_grad).wait()


def hand_kernel(grad, output, sums, o_grad, o_output, *refs):
    (low, wide, held), sems = refs[4:7], refs[7]
    gets, puts = [], []
    for n, (source, middle, last, target) in enumerate(
        ((grad, low, wide, o_grad), (output, held, held, o_output))
    ):
        rows = source.shape[0] // COPIES
        for c in range(COPIES):
            part = pl.ds(c * rows, rows)
            gets.append(pltpu.make_async_copy(source.at[part], middle.at[part], sems.at[0, n, c]))
            puts.append(pltpu.make_async_copy(last.at[part], target.at[part], sems.at[1, n, c]))
    for get in gets:
        get.start()
    for n, out in enumerate(refs[:4]):
        out[...] = sums[n, : out.shape[0]]
    for n, (get, put) in enumerate(zip(gets, puts)):
        get.wait()
        if n < COPIES:
            part = pl.ds(n * (grad.shape[0] // COPIES), grad.shape[0] // COPIES)
            wide[part, :] = low[part, :].astype(wide.dtype)
        put.start()
    for put in puts:
        put.wait()


def gather_kernel(slabs, stride, orders, *refs):
    count = len(orders)
    sources, targets = refs[:count], refs[count : 2 * count]
    own_sems, send_sems, recv_sems = refs[2 * count :]
    bits = slabs.bit_length() - 1
    place, core = lax.axis_index("dp"), lax.axis_index("tp")
    me = place // stride
    index = [(me // (1 << b)) % 2 for b in range(bits)]

    def partner(b):
        here = index[b]
        return (place + (1 - 2 * here) * ((1 << b) * stride), core)

    sibling = (place, 1 - core)
    barrier = pltpu.get_barrier_semaphore()
    for b in range(bits):
        pl.semaphore_signal(barrier, inc=1, device_id=partner(b), device_id_type=MESH)
    pl.semaphore_signal(barrier, inc=1, device_id=sibling, device_id_type=MESH)
    pl.semaphore_wait(barrier, bits + 1)

    def view(target, done):
        where = tuple(slice(None) if b in done else index[b] for b in reversed(range(bits)))
        return target.at[(core,) + where]

    owns, copies = [], {}
    for i in range(count):
        source = sources[i]
        own = pltpu.make_async_copy(source, view(targets[i], ()), own_sems.at[i])
        own.start()
        owns.append(own)

    def start(i, step):
        if step == 0:
            source, target, device = sources[i], view(targets[i], ()), partner(orders[i][0])
        elif step < bits:
            source = target = view(targets[i], orders[i][:step])
            device = partner(orders[i][step])
        else:
            source = target = targets[i].at[core]
            device = sibling
        copy = pltpu.make_async_remote_copy(
            src_ref=source,
            dst_ref=target,
            send_sem=send_sems.at[i, step],
            recv_sem=recv_sems.at[i, step],
            device_id=device,
            device_id_type=MESH,
        )
        copy.start()
        copies[i, step] = copy

    ahead = 2
    for tick in range(count + (bits + 1) * ahead + 1):
        for step in range(bits + 1, -1, -1):
            i = tick - step * ahead
            if 0 <= i < count:
                if step > 0:
                    copies[i, step - 1].wait_recv()
                if step == 1:
                    owns[i].wait()
                if step <= bits:
                    start(i, step)
    for copy in copies.values():
        copy.wait_send()


def gather_weights(shards, orders, slabs, stride):
    bits = slabs.bit_length() - 1
    count = len(shards)
    shapes = [
        jax.ShapeDtypeStruct((2,) + (2,) * bits + s.shape, s.dtype) for s in shards
    ]
    full = pl.pallas_call(
        functools.partial(gather_kernel, slabs, stride, orders),
        out_shape=shapes,
        in_specs=[pl.BlockSpec(memory_space=pl.ANY)] * count,
        out_specs=[pl.BlockSpec(memory_space=pl.ANY)] * count,
        scratch_shapes=[
            pltpu.SemaphoreType.DMA((count,)),
            pltpu.SemaphoreType.DMA((count, bits + 1)),
            pltpu.SemaphoreType.DMA((count, bits + 1)),
        ],
        compiler_params=pltpu.CompilerParams(collective_id=1, has_side_effects=True),
        name="gather_weights",
    )(*shards)
    return [f.reshape((2, slabs * s.shape[0], s.shape[1])) for f, s in zip(full, shards)]


def beside(full):
    return jnp.concatenate([full[0], full[1]], axis=1)


def total_kernel(groups, in_ref, out_ref, *refs):
    count = len(groups)
    buffers = refs[:count]
    sends, recvs = refs[count:]
    place, core = lax.axis_index("dp"), lax.axis_index("tp")

    def digit(bit):
        return core if bit < 0 else (place // (1 << bit)) % 2

    def peer(group, flip):
        there, other = place, core
        for n, bit in enumerate(group):
            if flip & (1 << n):
                if bit < 0:
                    other = 1 - core
                else:
                    there = there + (1 - 2 * digit(bit)) * (1 << bit)
        return (there, other)

    barrier = pltpu.get_barrier_semaphore()
    signals = 0
    for group in groups:
        for flip in range(1, 1 << len(group)):
            pl.semaphore_signal(
                barrier, inc=1, device_id=peer(group, flip), device_id_type=MESH
            )
            signals += 1
    pl.semaphore_wait(barrier, signals)

    value = in_ref[...]
    sem, started = 0, []
    for group, buffer in zip(groups, buffers):
        mine = sum(digit(bit) * (1 << n) for n, bit in enumerate(group))
        buffer[mine] = value
        copies = []
        for flip in range(1, 1 << len(group)):
            copy = pltpu.make_async_remote_copy(
                src_ref=buffer.at[mine],
                dst_ref=buffer.at[mine],
                send_sem=sends.at[sem],
                recv_sem=recvs.at[sem],
                device_id=peer(group, flip),
                device_id_type=MESH,
            )
            copy.start()
            copies.append(copy)
            sem += 1
        for copy in copies:
            copy.wait_recv()
        started += copies
        value = buffer[0]
        for n in range(1, 1 << len(group)):
            value = value + buffer[n]
    out_ref[...] = value
    for copy in started:
        copy.wait_send()


def call_total(sums, n_dp):
    bits = n_dp.bit_length() - 1
    groups = [(-1, 0, 1)] + [tuple(range(b, min(b + 2, bits))) for b in range(2, bits, 2)]
    peers = sum((1 << len(g)) - 1 for g in groups)
    return pl.pallas_call(
        functools.partial(total_kernel, groups),
        out_shape=jax.ShapeDtypeStruct(sums.shape, sums.dtype),
        in_specs=[pl.BlockSpec(memory_space=pltpu.VMEM)],
        out_specs=pl.BlockSpec(memory_space=pltpu.VMEM),
        scratch_shapes=[pltpu.VMEM((1 << len(g),) + sums.shape, jnp.float32) for g in groups]
        + [pltpu.SemaphoreType.DMA((peers,)), pltpu.SemaphoreType.DMA((peers,))],
        compiler_params=pltpu.CompilerParams(collective_id=2, has_side_effects=True),
        name="total",
    )(sums)


SCORES, MIX, MIX_BACK = "qhe,khe->hqk", "hqk,khe->qhe", "hqk,qhe->khe"


def masked_scores(queries, keys, segments):
    raw = jnp.einsum(SCORES, queries, keys, preferred_element_type=jnp.float32)
    same = segments[:, None] == segments[None, :]
    return jnp.where(same[None, :, :], raw, MASKED)


def attend_forward(parts):
    queries, keys, values, segments = parts
    scores = masked_scores(queries, keys, segments)
    top = jnp.max(scores, axis=-1, keepdims=True)
    powers = jnp.exp(scores - top)
    total = jnp.sum(powers, axis=-1, keepdims=True)
    weights_low = (powers / total).astype(jnp.bfloat16)
    mixed = jnp.einsum(MIX, weights_low, values, preferred_element_type=jnp.float32)
    return mixed.astype(jnp.bfloat16), (top + jnp.log(total))[:, :, 0]


def attend_backward(parts):
    queries, keys, values, segments, logsum, mixed_grad = parts
    bf16, f32 = jnp.bfloat16, jnp.float32
    scores = masked_scores(queries, keys, segments)
    probs = jnp.exp(scores - logsum[:, :, None])
    value_grad = jnp.einsum(MIX_BACK, probs.astype(bf16), mixed_grad, preferred_element_type=f32)
    prob_grad = jnp.einsum(SCORES, mixed_grad, values, preferred_element_type=f32)
    total = jnp.sum(probs * prob_grad, axis=-1, keepdims=True)
    score_grad = (probs * (prob_grad - total)).astype(bf16)
    query_grad = jnp.einsum(MIX, score_grad, keys, preferred_element_type=f32)
    key_grad = jnp.einsum(MIX_BACK, score_grad, queries, preferred_element_type=f32)
    query_grad = query_grad * (1.0 / math.sqrt(HD))
    return query_grad.astype(bf16), key_grad.astype(bf16), value_grad.astype(bf16)


def whole_sequences(a, w):
    bf16 = jnp.bfloat16
    tokens, segments = a.tokens, a.segments
    rows, model = tokens.shape
    queries = (dot(tokens, w.query) * (1.0 / math.sqrt(HD))).astype(bf16)
    keys = dot(tokens, w.key).astype(bf16)
    values = dot(tokens, w.value).astype(bf16)
    split = (segments.shape[0], SEQ_LEN, model // HD, HD)
    blocks = [x.reshape(split) for x in (queries, keys, values)] + [segments]
    mixed, logsum = lax.map(attend_forward, tuple(blocks))
    attention = dot_nt(mixed.reshape(rows, model), w.out_t)
    normed_one, inverse_one = normalize(tokens.astype(jnp.float32) + attention)
    hidden = normed_one * a.gain_one
    branch, slopes = 0.0, []
    for w_in, ff_t in ((w.w_in, w.ff_t),):
        inner, back = jax.vjp(
            lambda x: jax.nn.gelu(x, approximate=False), dot(hidden.astype(bf16), w_in)
        )
        slopes.append(back)
        branch = branch + dot_nt(inner.astype(bf16), ff_t)
    normed_two, inverse_two = normalize(hidden + branch)
    output = (normed_two * a.gain_two).astype(bf16)
    grad = norm_back(a.cotangent.astype(jnp.float32) * a.gain_two, normed_two, inverse_two)
    low = grad.astype(bf16)
    for w_in, ff_t, back in ((w.w_in, w.ff_t, slopes[0]),):
        grad = grad + dot_nt(back(dot(low, ff_t))[0].astype(bf16), w_in)
    sum_one = norm_back(grad * a.gain_one, normed_one, inverse_one)
    mixed_grad = dot(sum_one.astype(bf16), w.out_t).astype(bf16)
    grads = lax.map(attend_backward, tuple(blocks) + (logsum, mixed_grad.reshape(split)))
    query_grad, key_grad, value_grad = [g.reshape(rows, model) for g in grads]
    token_grad = sum_one + dot_nt(query_grad, w.query) + dot_nt(key_grad, w.key)
    token_grad = token_grad + dot_nt(value_grad, w.value)
    low = dot(tokens, w.down).astype(bf16)
    sums = []
    for scale, bias, grad in (
        (a.query_scale, a.query_bias, query_grad),
        (a.value_scale, a.value_bias, value_grad),
    ):
        product = dot_tn(low, grad) * w.up.astype(jnp.float32)
        sums.append(jnp.sum(product * bias, axis=1))
        over = jnp.sum(product * scale[:, None], axis=0)
        sums.append(jnp.pad(over, (0, low.shape[1] - model)))
    return output, token_grad, jnp.stack(sums)


def call_layer(stride, bits, n_dp, a, rows):
    model = a.tokens.shape[1]
    slab, width = a.w_query.shape
    quarters = a.w_in.shape[1] // width
    ranks = a.down.shape[1]
    seqs, pairs = rows // SEQ_LEN, model // LANES
    bf16, f32 = jnp.bfloat16, jnp.float32
    lead = (2,) * bits
    square = lead + (slab, model)
    up_shape = lead + (a.up.shape[0], model)
    all_bits = n_dp.bit_length() - 1
    groups = [(-1, 0, 1)] + [tuple(range(b, min(b + 2, all_bits))) for b in range(2, all_bits, 2)]
    peers = sum((1 << len(g)) - 1 for g in groups)

    hbm = dict(
        tokens=a.tokens,
        cotangent=a.cotangent,
        w_key=a.w_key,
        out_t=a.out_t,
        w_in=a.w_in,
        ff_t=a.ff_t,
        up=a.up,
    )
    vmem = dict(
        segments=a.segments,
        w_query=a.w_query,
        w_value=a.w_value,
        down=a.down,
        gain_one=a.gain_one,
        gain_two=a.gain_two,
        query_scale=a.query_scale,
        query_bias=a.query_bias,
        value_scale=a.value_scale,
        value_bias=a.value_bias,
    )
    outs = dict(o_output=((rows, model), bf16), o_grad=((rows, model), bf16))
    kept = dict(o_sums=((4, ranks), f32), o_flag=((1, 1), f32))
    scratch = dict(
        up_full=(up_shape, bf16),
        qkv_full=(lead + (slab, 3 * model), bf16),
        out_full=(square, bf16),
        down_full=(lead + (slab, ranks), bf16),
        win=(lead + (slab, quarters * model), bf16),
        wout=(lead + (slab, quarters * model), bf16),
        query_own=((slab, width), bf16),
        value_own=((slab, width), bf16),
        raw=((rows, model), bf16),
        tok=((rows, model), bf16),
        turn=((seqs, SEQ_LEN, SEQ_LEN), bf16),
        same=((seqs, SPAN, SPAN), f32),
        lowest=((8, 2 * SPAN), f32),
        probs=((pairs, 2 * seqs, SPAN, 2 * SPAN), bf16),
        queries=((rows, model), bf16),
        keys=((rows, model), bf16),
        values=((rows, model), bf16),
        mixed=((rows, model), bf16),
        normed=((rows, model), f32),
        inverse=((rows, LANES), f32),
        hidden=((rows, model), bf16),
        inner=((rows, quarters * model), bf16),
        slope=((rows, quarters * model), bf16),
        wide=((rows, model), f32),
        sums=((4, ranks), f32),
    )
    sems = dict(
        own_sems=(len(PIECES),),
        send_sems=(len(PIECES), bits + 1),
        recv_sems=(len(PIECES), bits + 1),
        total_sends=(peers,),
        total_recvs=(peers,),
        in_sems=(2,),
        out_sems=(2, seqs),
    )
    names = tuple(hbm) + tuple(vmem) + tuple(outs) + tuple(kept) + tuple(scratch) + tuple(sems)
    results = pl.pallas_call(
        functools.partial(layer_kernel, stride, bits, groups, names),
        out_shape=[jax.ShapeDtypeStruct(*v) for v in (outs | kept).values()],
        in_specs=[pl.BlockSpec(memory_space=pl.ANY)] * len(hbm)
        + [pl.BlockSpec(memory_space=pltpu.VMEM)] * len(vmem),
        out_specs=[pl.BlockSpec(memory_space=pl.ANY)] * len(outs)
        + [pl.BlockSpec(memory_space=pltpu.VMEM)] * len(kept),
        scratch_shapes=[pltpu.VMEM(*v) for v in scratch.values()]
        + [pltpu.SemaphoreType.DMA(v) for v in sems.values()]
        + [pltpu.VMEM((1 << len(g), 4, ranks), f32) for g in groups],
        compiler_params=pltpu.CompilerParams(
            collective_id=0, has_side_effects=True, vmem_limit_bytes=VMEM_LIMIT
        ),
        name="layer",
    )(*hbm.values(), *vmem.values())
    return results


def call_hand(output, grad, sums):
    f32 = jnp.float32
    ranks, (rows, model) = sums.shape[1], grad.shape
    grad, output, *totals = pl.pallas_call(
        hand_kernel,
        out_shape=[
            jax.ShapeDtypeStruct(grad.shape, f32),
            jax.ShapeDtypeStruct(output.shape, output.dtype),
            jax.ShapeDtypeStruct((ranks,), f32),
            jax.ShapeDtypeStruct((model,), f32),
            jax.ShapeDtypeStruct((ranks,), f32),
            jax.ShapeDtypeStruct((model,), f32),
        ],
        in_specs=[pl.BlockSpec(memory_space=pl.ANY)] * 2 + [pl.BlockSpec(memory_space=pltpu.VMEM)],
        out_specs=[pl.BlockSpec(memory_space=pl.ANY)] * 2
        + [pl.BlockSpec(memory_space=pltpu.VMEM)] * 4,
        scratch_shapes=[
            pltpu.VMEM(grad.shape, grad.dtype),
            pltpu.VMEM(grad.shape, f32),
            pltpu.VMEM(output.shape, output.dtype),
            pltpu.SemaphoreType.DMA((2, 2, COPIES)),
        ],
        compiler_params=pltpu.CompilerParams(vmem_limit_bytes=VMEM_LIMIT),
        name="hand",
    )(grad, output, sums)
    return (output, grad) + tuple(totals)


def per_device(
    n_dp,
    tokens,
    segment_ids,
    cotangent,
    w_query,
    w_key,
    w_value,
    w_output,
    shared_down,
    shared_up,
    w_in,
    w_out,
    gain_one,
    gain_two,
    query_scale,
    query_bias,
    value_scale,
    value_bias,
):
    rows, model = tokens.shape[0] // 2, tokens.shape[1]
    ranks = shared_down.shape[1]
    shards = dict(
        w_query=w_query,
        w_key=w_key,
        w_value=w_value,
        out_t=w_output.T,
        down=shared_down,
        up=shared_up,
        w_in=w_in,
        ff_t=w_out.T,
    )
    stride = n_dp // SLABS
    if stride > 1:
        groups = [list(range(g * stride, (g + 1) * stride)) for g in range(SLABS)]
        gather = functools.partial(lax.all_gather, axis=0, tiled=True, axis_index_groups=groups)
        shards = {n: gather(s, "dp") for n, s in shards.items()}
    arrays = types.SimpleNamespace(
        **shards,
        tokens=tokens,
        cotangent=cotangent,
        segments=segment_ids,
        gain_one=gain_one,
        gain_two=gain_two,
        query_scale=query_scale,
        query_bias=query_bias,
        value_scale=value_scale,
        value_bias=value_bias,
    )
    bits = SLABS.bit_length() - 1
    output, grad, sums, flag = call_layer(stride, bits, n_dp, arrays, rows)
    def halves():
        return call_hand(output, grad, sums)

    def whole():
        core = lax.axis_index("tp")
        own = types.SimpleNamespace(**vars(arrays))
        own.tokens = lax.dynamic_slice_in_dim(tokens, core * rows, rows, 0)
        own.cotangent = lax.dynamic_slice_in_dim(cotangent, core * rows, rows, 0)
        count = segment_ids.shape[0] // 2
        own.segments = lax.dynamic_slice_in_dim(segment_ids, core * count, count, 0)
        half = lax.dynamic_slice_in_dim(arrays.down, core * (ranks // 2), ranks // 2, 1)
        names = ("query", "key", "value", "out_t", "up", "down", "w_in", "ff_t")
        mine = [arrays.w_query, arrays.w_key, arrays.w_value, arrays.out_t, arrays.up, half]
        mine += [arrays.w_in, arrays.ff_t]
        order = tuple(range(bits - 1, -1, -1))
        full = gather_weights(mine, [order] * len(mine), SLABS, stride)
        full = [jnp.concatenate([f[0], f[1]], axis=1) for f in full]
        weights = types.SimpleNamespace(**dict(zip(names, full)))
        for scale, bias, name in (
            (query_scale, query_bias, "query"),
            (value_scale, value_bias, "value"),
        ):
            extra = dot((weights.down * scale).astype(jnp.bfloat16), weights.up) * bias
            setattr(weights, name, (getattr(weights, name) + extra).astype(jnp.bfloat16))
        output, token_grad, parts = whole_sequences(own, weights)
        return call_hand(output, token_grad, call_total(parts, n_dp))

    return lax.cond(flag[0, 0] == 0.0, halves, whole)


def solution(mesh):
    in_specs = (
        P("dp", None),
        P("dp", None),
        P("dp", None),
        P("dp", "tp"),
        P("dp", "tp"),
        P("dp", "tp"),
        P("tp", "dp"),
        P("dp", None),
        P("dp", "tp"),
        P("dp", "tp"),
        P("tp", "dp"),
        P(),
        P(),
        P(),
        P(),
        P(),
        P(),
    )
    out_specs = (P(("dp", "tp"), None), P(("dp", "tp"), None), P(), P(), P(), P())
    return jax.shard_map(
        functools.partial(per_device, mesh.shape["dp"]),
        mesh=mesh,
        in_specs=in_specs,
        out_specs=out_specs,
        check_vma=False,
    )
```

```python
import functools
import math
import types

import jax
import jax.numpy as jnp
from jax import lax
from jax.experimental import pallas as pl
from jax.experimental.pallas import tpu as pltpu
from jax.sharding import PartitionSpec as P

HD = 64
SEQ_LEN = 512
SPAN = SEQ_LEN // 2
LABELS = 8
LANES = 128
SLABS = 16
COPIES = 4
MASKED = -1000000000.0
MESH = pl.DeviceIdType.MESH
VMEM_LIMIT = 62 << 20


def dot(left, right):
    return jnp.dot(left, right, preferred_element_type=jnp.float32)


def dot_nt(left, right):
    return lax.dot_general(
        left, right, (((1,), (1,)), ((), ())), preferred_element_type=jnp.float32
    )


def dot_tn(left, right):
    return lax.dot_general(
        left, right, (((0,), (0,)), ((), ())), preferred_element_type=jnp.float32
    )


def normalize(values):
    average = jnp.mean(values, axis=-1, keepdims=True)
    centered = values - average
    variance = jnp.mean(centered * centered, axis=-1, keepdims=True)
    inverse = lax.rsqrt(variance + 1e-05)
    return centered * inverse, inverse


def norm_back(scaled, normed, inverse):
    first = jnp.mean(scaled, axis=-1, keepdims=True)
    second = jnp.mean(scaled * normed, axis=-1, keepdims=True)
    return inverse * (scaled - first - normed * second)


def gelu_and_slope(values):
    below = 0.5 * lax.erf(values * (1.0 / math.sqrt(2.0))) + 0.5
    bell = jnp.exp(values * values * -0.5) * (1.0 / math.sqrt(2.0 * math.pi))
    return values * below, below + values * bell


def own_lanes(pair):
    lane = lax.broadcasted_iota(jnp.int32, pair.shape, 1)
    zeros = jnp.zeros_like(pair)
    return jnp.concatenate([jnp.where(lane < HD, pair, zeros), jnp.where(lane < HD, zeros, pair)])


def join_heads(wide):
    n = wide.shape[1] // 2
    return jnp.concatenate([wide[:HD, :n], wide[HD:, n:]]).T


def label_rows(row):
    kind = lax.broadcasted_iota(jnp.int32, (LABELS, SEQ_LEN), 0)
    hot = jnp.where(kind == row, 1.0, 0.0)
    many = jnp.sum(hot, axis=1, keepdims=True)
    which = lax.broadcasted_iota(jnp.int32, (LABELS, 1), 0)
    first = jnp.min(jnp.where(many == float(SPAN), which, LABELS), axis=0, keepdims=True)
    start = jnp.sum(jnp.where(row < first, 1, 0), axis=1, keepdims=True)
    return hot, start


def roll_matrix(start, back):
    here = lax.broadcasted_iota(jnp.int32, (SEQ_LEN, SEQ_LEN), 1 if back else 0)
    there = lax.broadcasted_iota(jnp.int32, (SEQ_LEN, SEQ_LEN), 0 if back else 1)
    moved = here + start
    moved = jnp.where(moved >= SEQ_LEN, moved - SEQ_LEN, moved)
    return jnp.where(moved == there, 1.0, 0.0).astype(jnp.bfloat16)


PIECES = ((0, 0), (0, 4), (0, 1), (1, 1), (1, 1), (1, 1), (2, 1), (2, 1), (2, 6), (3, 4), (3, 0), (3, 0), (4, 3), (6, 1), (7, 1), (8, 1), (9, 7), (10, 5), (11, 7), (12, 1), (13, 6), (5, 1))
PLAN = (
    (0, (24, 16, 0, 8, 40, 32, 25, 1, 112, 104, 9, 17)),
    (1, (10, 41, 26, 136, 33, 2, 144, 128, 18, 96, 11, 27, 3, 42, 34, 120, 19, 160, 43, 97, 145, 12, 129, 113, 137, 20, 35, 4)),
    (-1, (88, 48, 64, 80, 72, 56, 49, 65, 89, 81, 73, 57, 50, 66, 74, 58, 82, 90, 152, 121, 105, 114, 75, 36, 59, 91, 44, 98, 67, 83, 28, 29, 37, 45)),
    (7, {1: (51, 60, 153, 106, 76, 115, 68)}),
    (-1, (130, 122, 52, 53, 61, 69)),
    (8, {1: (168, 107, 92, 99, 161, 154, 138, 84)}),
    (-1, (77, 85, 93)),
    (9, {1: (123, 146)}),
    (0, {3: (116, 131), 4: (162,), 5: (100, 139)}),
    (-1, (108, 101)),
    (1, {1: (169, 147, 155)}),
    (-1, (109,)),
    (2, {3: (163, 124), 4: (132, 117), 8: (125,), 10: (140,), 11: (156,), 12: (133,), 13: (148, 170)}),
    (-1, (141, 149, 157)),
    (3, {3: (164,)}),
    (2, ()),
    (-1, (171, 165)),
    (4, {6: (172,)}),
    (-1, (5, 13, 21)),
    (5, {}),
    (-1, (173,)),
    (6, {}),
)


def layer_kernel(stride, bits, groups, names, *refs):
    r = types.SimpleNamespace(**dict(zip(names, refs)))
    buffers = refs[len(names) :]
    place, core = lax.axis_index("dp"), lax.axis_index("tp")
    me = place // stride
    index = [(me // (1 << b)) % 2 for b in range(bits)]
    width = r.w_query.shape[1]
    rows, model = r.tok.shape
    quarters = r.win.shape[-1] // model
    seqs = rows // SEQ_LEN
    pairs = 2 * width // LANES
    bf16 = jnp.bfloat16

    def partner(b):
        return (place + (1 - 2 * index[b]) * ((1 << b) * stride), core)

    sibling = (place, 1 - core)

    top, rest = [bits - 1], list(range(bits - 2, 1, -1))
    orders = (
        top + rest + [1, 0],
        top + rest + [0, 1],
        [0, 1] + top + rest,
        [1, 0] + top + rest,
        top + [0, 1] + rest,
        top + [1, 0] + rest,
        top + [0] + rest + [1],
        top + [1] + rest + [0],
    )
    ranks = r.down.shape[1]
    half_rank = ranks // 2
    shards = [
        (r.up, r.up_full, width, 0, 0),
        (r.w_key, r.qkv_full, width, 0, model),
        (r.query_own, r.qkv_full, width, 0, 0),
        (r.value_own, r.qkv_full, width, 0, 2 * model),
        (r.out_t, r.out_full, width, 0, 0),
        (r.h_down, r.down_full, half_rank, core * half_rank, 0),
    ]
    shards += [(r.w_in, r.win, width, j * width, j * model) for j in range(quarters)]
    shards += [(r.ff_t, r.wout, width, j * width, j * model) for j in range(quarters)]
    seen, pieces = {}, []
    for name, order in PIECES:
        seen[name] = seen.get(name, 0) + 1
    taken = {}
    for name, order in PIECES:
        source, target, columns, offset, base = shards[name]
        part = columns // seen[name]
        at = taken.get(name, 0)
        taken[name] = at + 1
        first = offset + at * part
        if not isinstance(first, int):
            first = pl.multiple_of(first, LANES)
        spot = pl.ds(pl.multiple_of(core * columns + base + at * part, LANES), part)
        pieces.append((source.at[:, pl.ds(first, part)], target, spot, orders[order]))

    def view(i, done):
        where = tuple(slice(None) if b in done else index[b] for b in reversed(range(bits)))
        return pieces[i][1].at[where + (slice(None), pieces[i][2])]

    def own(i):
        return pltpu.make_async_copy(pieces[i][0], view(i, ()), r.own_sems.at[i])

    def remote(i, step):
        source, _, _, order = pieces[i]
        there = view(i, order[:step])
        return pltpu.make_async_remote_copy(
            src_ref=source if step == 0 else there,
            dst_ref=there,
            send_sem=r.send_sems.at[i, step],
            recv_sem=r.recv_sems.at[i, step],
            device_id=partner(order[step]) if step < bits else sibling,
            device_id_type=MESH,
        )

    def move(i, step):
        if step > 0:
            remote(i, step - 1).wait_recv()
        if step == 0:
            own(i).start()
        if step == 1:
            own(i).wait()
        if step <= bits:
            remote(i, step).start()

    def fetch(n, source, target):
        return pltpu.make_async_copy(source, target, r.in_sems.at[n])

    small = (r.segments, r.w_query, r.w_value, r.down, r.query_scale, r.query_bias)
    small += (r.value_scale, r.value_bias, r.gain_one, r.gain_two)
    given = (r.h_segments, r.h_w_query, r.h_w_value, r.h_down, r.h_query_scale, r.h_query_bias)
    given += (r.h_value_scale, r.h_value_bias, r.h_gain_one, r.h_gain_two)
    get_small = [fetch(2 + n, a, b) for n, (a, b) in enumerate(zip(given, small))]

    mine = pl.ds(pl.multiple_of(core * rows, rows), rows)
    get_tokens = fetch(0, r.tokens.at[mine], r.raw)
    get_cotangent = fetch(1, r.cotangent.at[mine], r.raw)

    def seq_rows(s):
        return pl.ds(pl.multiple_of(s * SEQ_LEN, SEQ_LEN), SEQ_LEN)

    def full(ref, first=0, count=None):
        value = ref[..., pl.ds(first, count or ref.shape[-1])]
        return value.reshape((value.shape[-2] * (1 << bits), value.shape[-1]))

    def prep():
        get_tokens.wait()
        for copy in get_small:
            copy.wait()
        every = r.segments[...]
        held = jnp.where(core == 0, every[:seqs], every[seqs:])
        found = []
        for s in range(seqs):
            hot, start = label_rows(held[s : s + 1])
            turn = roll_matrix(start, False)
            r.turn[s] = turn
            part = pl.ds(s * SEQ_LEN, SEQ_LEN)
            r.tok[part, :] = dot(turn, r.raw[part, :]).astype(bf16)
            turned = dot_nt(hot.astype(bf16), turn)[:, SPAN:]
            r.same[s] = dot_tn(turned, turned)
            found.append(jnp.where(start < SEQ_LEN, 0.0, MASKED))
        lowest = functools.reduce(jnp.minimum, found)
        r.lowest[...] = jnp.broadcast_to(lowest, r.lowest.shape)
        get_cotangent.start()

    def merge():
        columns = pl.ds(pl.multiple_of(core * width, width), width)
        up_half = r.up_full[..., columns]
        up_half = up_half.reshape((up_half.shape[-2] * (1 << bits), width))
        down = r.down[...].astype(jnp.float32)
        for scale, bias, weight, target in (
            (r.query_scale, r.query_bias, r.w_query, r.query_own),
            (r.value_scale, r.value_bias, r.w_value, r.value_own),
        ):
            scaled = (down * scale[...][None, :]).astype(bf16)
            extra = dot(scaled, up_half) * bias[columns][None, :]
            target[...] = (weight[...].astype(jnp.float32) + extra).astype(bf16)

    def project(first, target, factor):
        def body(s, hook):
            hook(0)
            value = dot(r.tok[seq_rows(s), :], full(r.qkv_full, first, model))
            target[seq_rows(s), :] = (value * factor).astype(bf16)

        return body

    quads = [(s, half) for s in range(seqs) for half in range(2)]

    def masked(scores, s, half):
        if half == 0:
            return scores
        same = r.same[s] > 0.5
        return jnp.where(jnp.concatenate([same, same], axis=1), scores, MASKED)

    places = [pl.ds(s * SEQ_LEN + half * SPAN, SPAN) for s, half in quads]

    def attend(p, hook):
        hook(0)
        columns = pl.ds(pl.multiple_of(p * LANES, LANES), LANES)
        scores = [
            dot_nt(r.keys[here, columns], own_lanes(r.queries[here, columns])) for here in places
        ]
        for n, (s, half) in enumerate(quads):
            score = masked(scores[n], s, half)
            top = jnp.max(score, axis=0, keepdims=True)
            power = jnp.exp(score - top)
            total = jnp.sum(power, axis=0, keepdims=True)
            r.lowest[n : n + 1, :] = jnp.minimum(r.lowest[n : n + 1, :], top)
            r.probs[p, n] = (power * (1.0 / total)).astype(bf16)
        for n, here in enumerate(places):
            mixed = dot(r.values[here, columns].T, r.probs[p, n])
            r.mixed[here, columns] = join_heads(mixed).astype(bf16)

    def attend_back(_, hook):
        blocks = [(p, n) for p in range(pairs) for n in range(len(quads))]
        fronts, lows = {}, {}

        def front(p, n):
            columns = pl.ds(p * LANES, LANES)
            grads = own_lanes(r.mixed[places[n], columns])
            return grads, dot_nt(r.values[places[n], columns], grads)

        def middle(p, n):
            prob = r.probs[p, n].astype(jnp.float32)
            both = prob * fronts[p, n][1]
            total = jnp.sum(both, axis=0, keepdims=True)
            return (both - prob * total).astype(bf16)

        def back(p, n):
            columns = pl.ds(p * LANES, LANES)
            value_grad = dot(r.probs[p, n], fronts[p, n][0])
            key_grad = dot(lows[p, n], own_lanes(r.queries[places[n], columns]))
            query_grad = join_heads(dot(r.keys[places[n], columns].T, lows[p, n]))
            query_grad = query_grad * (1.0 / math.sqrt(HD))
            for a, grad in enumerate((query_grad, key_grad, value_grad)):
                r.inner[places[n], pl.ds(a * model + p * LANES, LANES)] = grad.astype(bf16)

        for at in range(len(blocks) + 2):
            if at % len(quads) == 0 and at < len(blocks):
                hook(at // len(quads))
            if at < len(blocks):
                fronts[blocks[at]] = front(*blocks[at])
            if 1 <= at <= len(blocks):
                lows[blocks[at - 1]] = middle(*blocks[at - 1])
            if at >= 2:
                back(*blocks[at - 2])

    def parts(s, count):
        size = SEQ_LEN // count
        return [
            pl.ds(pl.multiple_of(s * SEQ_LEN + n * size, size), size) for n in range(count)
        ]

    def first_norm(s, hook):
        for n, here in enumerate(parts(s, 2)):
            hook(n)
            attention = dot_nt(r.mixed[here, :], full(r.out_full))
            normed, inverse = normalize(r.tok[here, :].astype(jnp.float32) + attention)
            r.normed[here, :] = normed
            r.inverse[here, :] = jnp.broadcast_to(inverse, (inverse.shape[0], LANES))
            r.hidden[here, :] = (normed * r.gain_one[...][None, :]).astype(bf16)

    def widen(it, hook):
        j, s = it // seqs, it % seqs
        columns = pl.ds(pl.multiple_of(j * model, model), model)
        hook(0)
        weight = r.win[..., columns]
        weight = weight.reshape((model, model))
        for n, here in enumerate(parts(s, SEQ_LEN // LANES)):
            if n == SEQ_LEN // LANES // 2:
                hook(1)
            inner, slope = gelu_and_slope(dot(r.hidden[here, :], weight))
            r.inner[here, columns] = inner.astype(bf16)
            r.slope[here, columns] = slope.astype(bf16)

    most = (quarters - 1) * model

    def narrow(s, hook):
        for n, here in enumerate(parts(s, 2)):
            hook(n)
            r.wide[here, :] = dot_nt(r.inner[here, :most], full(r.wout, 0, most))

    def second_norm(s, hook):
        gain_one, gain_two = r.gain_one[...][None, :], r.gain_two[...][None, :]
        halves = parts(s, 2)
        grads, lows = [], []
        hook(0)
        for here in halves:
            branch = r.wide[here, :] + dot_nt(r.inner[here, most:], full(r.wout, most, model))
            normed, inverse = normalize(r.normed[here, :] * gain_one + branch)
            r.hidden[here, :] = (normed * gain_two).astype(bf16)
            grad = norm_back(r.raw[here, :].astype(jnp.float32) * gain_two, normed, inverse)
            grads.append(grad)
            lows.append(grad.astype(bf16))
        for j in range(quarters):
            if j:
                hook(j)
            part = pl.ds(j * model, model)
            inner = [
                dot(low, full(r.wout, j * model, model)) * r.slope[here, part].astype(jnp.float32)
                for low, here in zip(lows, halves)
            ]
            grads = [
                grad + dot_nt(one.astype(bf16), full(r.win, j * model, model))
                for grad, one in zip(grads, inner)
            ]
        for grad, here in zip(grads, halves):
            back = norm_back(grad * gain_one, r.normed[here, :], r.inverse[here, :][:, :1])
            r.wide[here, :] = back
            r.mixed[here, :] = dot(back.astype(bf16), full(r.out_full)).astype(bf16)

    def cotangents():
        get_cotangent.wait()
        for s in range(seqs):
            here = pl.ds(s * SEQ_LEN, SEQ_LEN)
            r.raw[here, :] = dot(r.turn[s], r.raw[here, :]).astype(bf16)

    def rank(s, hook):
        hook(0)
        here = seq_rows(s)
        r.slope[here, :ranks] = dot(r.tok[here, :], full(r.down_full)).astype(bf16)

    def adapters(n, hook):
        block = ranks // 2
        part = pl.ds(pl.multiple_of(n * block, block), block)
        low = r.slope[:, part]
        up = r.up_full[n].reshape((block, model)).astype(jnp.float32)
        kinds = ((0, 0, r.query_scale, r.query_bias), (2, 2 * model, r.value_scale, r.value_bias))
        products = [dot_tn(low, r.inner[:, first : first + model]) for _, first, _, _ in kinds]
        for product, (a, _, scales, bias) in zip(products, kinds):
            product = product * up
            scale = jnp.broadcast_to(scales[part][None, :], (LANES, block)).T
            r.sums[a + 1 : a + 2, :model] += jnp.sum(product * scale[:, :1], axis=0, keepdims=True)
            over = jnp.sum(product * bias[...][None, :], axis=1, keepdims=True)
            r.sums[a : a + 1, part] = jnp.broadcast_to(over, (block, LANES)).T[:1]

    def finish(s):
        here = seq_rows(s)
        grad = r.wide[here, :] + dot_nt(r.inner[here, : 3 * model], full(r.qkv_full))
        r.mixed[here, :] = dot_tn(r.turn[s], grad.astype(bf16)).astype(bf16)

    def give(n, s, source, target):
        part = pl.ds(s * SEQ_LEN, SEQ_LEN)
        return pltpu.make_async_copy(source.at[part], target.at[part], r.out_sems.at[n, s])

    def peer(group, flip):
        there, other = place, core
        for n, bit in enumerate(group):
            if flip & (1 << n):
                if bit < 0:
                    other = 1 - core
                else:
                    there = there + (1 - 2 * ((place // (1 << bit)) % 2)) * (1 << bit)
        return (there, other)

    def spread(g):
        group, buffer = groups[g], buffers[g]
        digits = [core if bit < 0 else (place // (1 << bit)) % 2 for bit in group]
        mine = sum(digit * (1 << n) for n, digit in enumerate(digits))
        before = sum((1 << len(one)) - 1 for one in groups[:g])
        return [
            pltpu.make_async_remote_copy(
                src_ref=buffer.at[mine],
                dst_ref=buffer.at[mine],
                send_sem=r.total_sends.at[before + flip - 1],
                recv_sem=r.total_recvs.at[before + flip - 1],
                device_id=peer(group, flip),
                device_id_type=MESH,
            )
            for flip in range(1, 1 << len(group))
        ], mine

    def send_sums(g, value):
        copies, mine = spread(g)
        buffers[g][mine] = value
        for copy in copies:
            copy.start()

    def take_sums(g):
        for copy in spread(g)[0]:
            copy.wait_recv()
        value = buffers[g][0]
        for n in range(1, 1 << len(groups[g])):
            value = value + buffers[g][n]
        return value

    get_tokens.start()
    for copy in get_small:
        copy.start()
    barrier = pltpu.get_barrier_semaphore()
    near_by = [partner(b) for b in range(bits)] + [sibling]
    near_by += [peer(g, flip) for g in groups for flip in range(1, 1 << len(g))]
    for device in near_by:
        pl.semaphore_signal(barrier, inc=1, device_id=device, device_id_type=MESH)
    pl.semaphore_wait(barrier, len(near_by))

    loops = (
        (pairs, 1, attend),
        (seqs, 2, first_norm),
        (quarters * seqs, 2, widen),
        (seqs, 2, narrow),
        (seqs, quarters, second_norm),
        (1, pairs, attend_back),
        (seqs, 1, rank),
        (seqs, 1, project(model, r.keys, 1.0)),
        (seqs, 1, project(0, r.queries, 1.0 / math.sqrt(HD))),
        (seqs, 1, project(2 * model, r.values, 1.0)),
    )
    blocks = (prep, merge, cotangents)

    def run_loop(count, spots, body, inside):
        def step(it, _):
            def hook(spot):
                for when, some in inside.items():
                    if when % spots != spot:
                        continue

                    @pl.when(it == when // spots)
                    def _(some=some):
                        for one in some:
                            move(one // 8, one % 8)

            body(it, hook)
            return 0

        def once(spot):
            for one in inside.get(spot, ()):
                move(one // 8, one % 8)

        if count == 1:
            body(0, once)
        else:
            lax.fori_loop(0, count, step, 0)

    for block, moves in PLAN:
        if isinstance(moves, tuple):
            for one in moves:
                move(one // 8, one % 8)
            if block >= 0:
                blocks[block]()
        else:
            run_loop(*loops[block], moves)

    r.sums[...] = jnp.zeros_like(r.sums)
    run_loop(2, 1, adapters, {})
    lowest = jnp.min(jnp.min(r.lowest[...], axis=1, keepdims=True), axis=0, keepdims=True)
    r.sums[1:2, model : model + LANES] = jnp.broadcast_to(
        jnp.where(lowest > 0.5 * MASKED, 0.0, 1.0), (1, LANES)
    )
    for g in range(len(groups)):
        send_sums(g, r.sums[...] if g == 0 else total)
        if g == 0:
            for s in range(seqs):
                here = seq_rows(s)
                r.raw[here, :] = dot_tn(r.turn[s], r.hidden[here, :]).astype(bf16)
                give(0, s, r.raw, r.o_output).start()
        if g < seqs:
            finish(g)
            give(1, g, r.mixed, r.o_grad).start()
        total = take_sums(g)
    r.o_sums[...] = total
    r.o_flag[...] = total[1:2, model : model + 1]
    for i in range(len(pieces)):
        for step in range(bits + 1):
            remote(i, step).wait_send()
    for g in range(len(groups)):
        for copy in spread(g)[0]:
            copy.wait_send()
    for s in range(seqs):
        give(0, s, r.raw, r.o_output).wait()
        give(1, s, r.mixed, r.o_grad).wait()


def hand_kernel(grad, output, sums, o_grad, o_output, *refs):
    (low, wide, held), sems = refs[4:7], refs[7]
    gets, puts = [], []
    for n, (source, middle, last, target) in enumerate(
        ((grad, low, wide, o_grad), (output, held, held, o_output))
    ):
        rows = source.shape[0] // COPIES
        for c in range(COPIES):
            part = pl.ds(c * rows, rows)
            gets.append(pltpu.make_async_copy(source.at[part], middle.at[part], sems.at[0, n, c]))
            puts.append(pltpu.make_async_copy(last.at[part], target.at[part], sems.at[1, n, c]))
    for get in gets:
        get.start()
    for n, out in enumerate(refs[:4]):
        out[...] = sums[n, : out.shape[0]]
    for n, (get, put) in enumerate(zip(gets, puts)):
        get.wait()
        if n < COPIES:
            part = pl.ds(n * (grad.shape[0] // COPIES), grad.shape[0] // COPIES)
            wide[part, :] = low[part, :].astype(wide.dtype)
        put.start()
    for put in puts:
        put.wait()


def gather_kernel(slabs, stride, orders, *refs):
    count = len(orders)
    sources, targets = refs[:count], refs[count : 2 * count]
    own_sems, send_sems, recv_sems = refs[2 * count :]
    bits = slabs.bit_length() - 1
    place, core = lax.axis_index("dp"), lax.axis_index("tp")
    me = place // stride
    index = [(me // (1 << b)) % 2 for b in range(bits)]

    def partner(b):
        here = index[b]
        return (place + (1 - 2 * here) * ((1 << b) * stride), core)

    sibling = (place, 1 - core)
    barrier = pltpu.get_barrier_semaphore()
    for b in range(bits):
        pl.semaphore_signal(barrier, inc=1, device_id=partner(b), device_id_type=MESH)
    pl.semaphore_signal(barrier, inc=1, device_id=sibling, device_id_type=MESH)
    pl.semaphore_wait(barrier, bits + 1)

    def view(target, done):
        where = tuple(slice(None) if b in done else index[b] for b in reversed(range(bits)))
        return target.at[(core,) + where]

    owns, copies = [], {}
    for i in range(count):
        source = sources[i]
        own = pltpu.make_async_copy(source, view(targets[i], ()), own_sems.at[i])
        own.start()
        owns.append(own)

    def start(i, step):
        if step == 0:
            source, target, device = sources[i], view(targets[i], ()), partner(orders[i][0])
        elif step < bits:
            source = target = view(targets[i], orders[i][:step])
            device = partner(orders[i][step])
        else:
            source = target = targets[i].at[core]
            device = sibling
        copy = pltpu.make_async_remote_copy(
            src_ref=source,
            dst_ref=target,
            send_sem=send_sems.at[i, step],
            recv_sem=recv_sems.at[i, step],
            device_id=device,
            device_id_type=MESH,
        )
        copy.start()
        copies[i, step] = copy

    ahead = 2
    for tick in range(count + (bits + 1) * ahead + 1):
        for step in range(bits + 1, -1, -1):
            i = tick - step * ahead
            if 0 <= i < count:
                if step > 0:
                    copies[i, step - 1].wait_recv()
                if step == 1:
                    owns[i].wait()
                if step <= bits:
                    start(i, step)
    for copy in copies.values():
        copy.wait_send()


def gather_weights(shards, orders, slabs, stride):
    bits = slabs.bit_length() - 1
    count = len(shards)
    shapes = [
        jax.ShapeDtypeStruct((2,) + (2,) * bits + s.shape, s.dtype) for s in shards
    ]
    full = pl.pallas_call(
        functools.partial(gather_kernel, slabs, stride, orders),
        out_shape=shapes,
        in_specs=[pl.BlockSpec(memory_space=pl.ANY)] * count,
        out_specs=[pl.BlockSpec(memory_space=pl.ANY)] * count,
        scratch_shapes=[
            pltpu.SemaphoreType.DMA((count,)),
            pltpu.SemaphoreType.DMA((count, bits + 1)),
            pltpu.SemaphoreType.DMA((count, bits + 1)),
        ],
        compiler_params=pltpu.CompilerParams(collective_id=1, has_side_effects=True),
        name="gather_weights",
    )(*shards)
    return [f.reshape((2, slabs * s.shape[0], s.shape[1])) for f, s in zip(full, shards)]


def beside(full):
    return jnp.concatenate([full[0], full[1]], axis=1)


def total_kernel(groups, in_ref, out_ref, *refs):
    count = len(groups)
    buffers = refs[:count]
    sends, recvs = refs[count:]
    place, core = lax.axis_index("dp"), lax.axis_index("tp")

    def digit(bit):
        return core if bit < 0 else (place // (1 << bit)) % 2

    def peer(group, flip):
        there, other = place, core
        for n, bit in enumerate(group):
            if flip & (1 << n):
                if bit < 0:
                    other = 1 - core
                else:
                    there = there + (1 - 2 * digit(bit)) * (1 << bit)
        return (there, other)

    barrier = pltpu.get_barrier_semaphore()
    signals = 0
    for group in groups:
        for flip in range(1, 1 << len(group)):
            pl.semaphore_signal(
                barrier, inc=1, device_id=peer(group, flip), device_id_type=MESH
            )
            signals += 1
    pl.semaphore_wait(barrier, signals)

    value = in_ref[...]
    sem, started = 0, []
    for group, buffer in zip(groups, buffers):
        mine = sum(digit(bit) * (1 << n) for n, bit in enumerate(group))
        buffer[mine] = value
        copies = []
        for flip in range(1, 1 << len(group)):
            copy = pltpu.make_async_remote_copy(
                src_ref=buffer.at[mine],
                dst_ref=buffer.at[mine],
                send_sem=sends.at[sem],
                recv_sem=recvs.at[sem],
                device_id=peer(group, flip),
                device_id_type=MESH,
            )
            copy.start()
            copies.append(copy)
            sem += 1
        for copy in copies:
            copy.wait_recv()
        started += copies
        value = buffer[0]
        for n in range(1, 1 << len(group)):
            value = value + buffer[n]
    out_ref[...] = value
    for copy in started:
        copy.wait_send()


def call_total(sums, n_dp):
    bits = n_dp.bit_length() - 1
    groups = [(-1, 0, 1)] + [tuple(range(b, min(b + 2, bits))) for b in range(2, bits, 2)]
    peers = sum((1 << len(g)) - 1 for g in groups)
    return pl.pallas_call(
        functools.partial(total_kernel, groups),
        out_shape=jax.ShapeDtypeStruct(sums.shape, sums.dtype),
        in_specs=[pl.BlockSpec(memory_space=pltpu.VMEM)],
        out_specs=pl.BlockSpec(memory_space=pltpu.VMEM),
        scratch_shapes=[pltpu.VMEM((1 << len(g),) + sums.shape, jnp.float32) for g in groups]
        + [pltpu.SemaphoreType.DMA((peers,)), pltpu.SemaphoreType.DMA((peers,))],
        compiler_params=pltpu.CompilerParams(collective_id=2, has_side_effects=True),
        name="total",
    )(sums)


SCORES, MIX, MIX_BACK = "qhe,khe->hqk", "hqk,khe->qhe", "hqk,qhe->khe"


def masked_scores(queries, keys, segments):
    raw = jnp.einsum(SCORES, queries, keys, preferred_element_type=jnp.float32)
    same = segments[:, None] == segments[None, :]
    return jnp.where(same[None, :, :], raw, MASKED)


def attend_forward(parts):
    queries, keys, values, segments = parts
    scores = masked_scores(queries, keys, segments)
    top = jnp.max(scores, axis=-1, keepdims=True)
    powers = jnp.exp(scores - top)
    total = jnp.sum(powers, axis=-1, keepdims=True)
    weights_low = (powers / total).astype(jnp.bfloat16)
    mixed = jnp.einsum(MIX, weights_low, values, preferred_element_type=jnp.float32)
    return mixed.astype(jnp.bfloat16), (top + jnp.log(total))[:, :, 0]


def attend_backward(parts):
    queries, keys, values, segments, logsum, mixed_grad = parts
    bf16, f32 = jnp.bfloat16, jnp.float32
    scores = masked_scores(queries, keys, segments)
    probs = jnp.exp(scores - logsum[:, :, None])
    value_grad = jnp.einsum(MIX_BACK, probs.astype(bf16), mixed_grad, preferred_element_type=f32)
    prob_grad = jnp.einsum(SCORES, mixed_grad, values, preferred_element_type=f32)
    total = jnp.sum(probs * prob_grad, axis=-1, keepdims=True)
    score_grad = (probs * (prob_grad - total)).astype(bf16)
    query_grad = jnp.einsum(MIX, score_grad, keys, preferred_element_type=f32)
    key_grad = jnp.einsum(MIX_BACK, score_grad, queries, preferred_element_type=f32)
    query_grad = query_grad * (1.0 / math.sqrt(HD))
    return query_grad.astype(bf16), key_grad.astype(bf16), value_grad.astype(bf16)


def whole_sequences(a, w):
    bf16 = jnp.bfloat16
    tokens, segments = a.tokens, a.segments
    rows, model = tokens.shape
    queries = (dot(tokens, w.query) * (1.0 / math.sqrt(HD))).astype(bf16)
    keys = dot(tokens, w.key).astype(bf16)
    values = dot(tokens, w.value).astype(bf16)
    split = (segments.shape[0], SEQ_LEN, model // HD, HD)
    blocks = [x.reshape(split) for x in (queries, keys, values)] + [segments]
    mixed, logsum = lax.map(attend_forward, tuple(blocks))
    attention = dot_nt(mixed.reshape(rows, model), w.out_t)
    normed_one, inverse_one = normalize(tokens.astype(jnp.float32) + attention)
    hidden = normed_one * a.gain_one
    branch, slopes = 0.0, []
    for w_in, ff_t in ((w.w_in, w.ff_t),):
        inner, back = jax.vjp(
            lambda x: jax.nn.gelu(x, approximate=False), dot(hidden.astype(bf16), w_in)
        )
        slopes.append(back)
        branch = branch + dot_nt(inner.astype(bf16), ff_t)
    normed_two, inverse_two = normalize(hidden + branch)
    output = (normed_two * a.gain_two).astype(bf16)
    grad = norm_back(a.cotangent.astype(jnp.float32) * a.gain_two, normed_two, inverse_two)
    low = grad.astype(bf16)
    for w_in, ff_t, back in ((w.w_in, w.ff_t, slopes[0]),):
        grad = grad + dot_nt(back(dot(low, ff_t))[0].astype(bf16), w_in)
    sum_one = norm_back(grad * a.gain_one, normed_one, inverse_one)
    mixed_grad = dot(sum_one.astype(bf16), w.out_t).astype(bf16)
    grads = lax.map(attend_backward, tuple(blocks) + (logsum, mixed_grad.reshape(split)))
    query_grad, key_grad, value_grad = [g.reshape(rows, model) for g in grads]
    token_grad = sum_one + dot_nt(query_grad, w.query) + dot_nt(key_grad, w.key)
    token_grad = token_grad + dot_nt(value_grad, w.value)
    low = dot(tokens, w.down).astype(bf16)
    sums = []
    for scale, bias, grad in (
        (a.query_scale, a.query_bias, query_grad),
        (a.value_scale, a.value_bias, value_grad),
    ):
        product = dot_tn(low, grad) * w.up.astype(jnp.float32)
        sums.append(jnp.sum(product * bias, axis=1))
        over = jnp.sum(product * scale[:, None], axis=0)
        sums.append(jnp.pad(over, (0, low.shape[1] - model)))
    return output, token_grad, jnp.stack(sums)


def call_layer(stride, bits, n_dp, a, rows):
    model = a.tokens.shape[1]
    slab, width = a.w_query.shape
    quarters = a.w_in.shape[1] // width
    ranks = a.down.shape[1]
    seqs, pairs = rows // SEQ_LEN, model // LANES
    bf16, f32 = jnp.bfloat16, jnp.float32
    lead = (2,) * bits
    square = lead + (slab, model)
    up_shape = lead + (a.up.shape[0], model)
    all_bits = n_dp.bit_length() - 1
    groups = [(-1, 0, 1)] + [tuple(range(b, min(b + 2, all_bits))) for b in range(2, all_bits, 2)]
    peers = sum((1 << len(g)) - 1 for g in groups)

    hbm = dict(
        tokens=a.tokens,
        cotangent=a.cotangent,
        w_key=a.w_key,
        out_t=a.out_t,
        w_in=a.w_in,
        ff_t=a.ff_t,
        up=a.up,
    )
    small = dict(
        segments=a.segments,
        w_query=a.w_query,
        w_value=a.w_value,
        down=a.down,
        gain_one=a.gain_one,
        gain_two=a.gain_two,
        query_scale=a.query_scale,
        query_bias=a.query_bias,
        value_scale=a.value_scale,
        value_bias=a.value_bias,
    )
    hbm |= {"h_" + n: v for n, v in small.items()}
    outs = dict(o_output=((rows, model), bf16), o_grad=((rows, model), bf16))
    kept = dict(o_sums=((4, ranks), f32), o_flag=((1, 1), f32))
    scratch = {n: (v.shape, v.dtype) for n, v in small.items()}
    scratch |= dict(
        up_full=(up_shape, bf16),
        qkv_full=(lead + (slab, 3 * model), bf16),
        out_full=(square, bf16),
        down_full=(lead + (slab, ranks), bf16),
        win=(lead + (slab, quarters * model), bf16),
        wout=(lead + (slab, quarters * model), bf16),
        query_own=((slab, width), bf16),
        value_own=((slab, width), bf16),
        raw=((rows, model), bf16),
        tok=((rows, model), bf16),
        turn=((seqs, SEQ_LEN, SEQ_LEN), bf16),
        same=((seqs, SPAN, SPAN), f32),
        lowest=((8, 2 * SPAN), f32),
        probs=((pairs, 2 * seqs, SPAN, 2 * SPAN), bf16),
        queries=((rows, model), bf16),
        keys=((rows, model), bf16),
        values=((rows, model), bf16),
        mixed=((rows, model), bf16),
        normed=((rows, model), f32),
        inverse=((rows, LANES), f32),
        hidden=((rows, model), bf16),
        inner=((rows, quarters * model), bf16),
        slope=((rows, quarters * model), bf16),
        wide=((rows, model), f32),
        sums=((4, ranks), f32),
    )
    sems = dict(
        own_sems=(len(PIECES),),
        send_sems=(len(PIECES), bits + 1),
        recv_sems=(len(PIECES), bits + 1),
        total_sends=(peers,),
        total_recvs=(peers,),
        in_sems=(2 + len(small),),
        out_sems=(2, seqs),
    )
    names = tuple(hbm) + tuple(outs) + tuple(kept) + tuple(scratch) + tuple(sems)
    results = pl.pallas_call(
        functools.partial(layer_kernel, stride, bits, groups, names),
        out_shape=[jax.ShapeDtypeStruct(*v) for v in (outs | kept).values()],
        in_specs=[pl.BlockSpec(memory_space=pl.ANY)] * len(hbm),
        out_specs=[pl.BlockSpec(memory_space=pl.ANY)] * len(outs)
        + [pl.BlockSpec(memory_space=pltpu.VMEM)] * len(kept),
        scratch_shapes=[pltpu.VMEM(*v) for v in scratch.values()]
        + [pltpu.SemaphoreType.DMA(v) for v in sems.values()]
        + [pltpu.VMEM((1 << len(g), 4, ranks), f32) for g in groups],
        compiler_params=pltpu.CompilerParams(
            collective_id=0, has_side_effects=True, vmem_limit_bytes=VMEM_LIMIT
        ),
        name="layer",
    )(*hbm.values())
    return results


def call_hand(output, grad, sums):
    f32 = jnp.float32
    ranks, (rows, model) = sums.shape[1], grad.shape
    grad, output, *totals = pl.pallas_call(
        hand_kernel,
        out_shape=[
            jax.ShapeDtypeStruct(grad.shape, f32),
            jax.ShapeDtypeStruct(output.shape, output.dtype),
            jax.ShapeDtypeStruct((ranks,), f32),
            jax.ShapeDtypeStruct((model,), f32),
            jax.ShapeDtypeStruct((ranks,), f32),
            jax.ShapeDtypeStruct((model,), f32),
        ],
        in_specs=[pl.BlockSpec(memory_space=pl.ANY)] * 2 + [pl.BlockSpec(memory_space=pltpu.VMEM)],
        out_specs=[pl.BlockSpec(memory_space=pl.ANY)] * 2
        + [pl.BlockSpec(memory_space=pltpu.VMEM)] * 4,
        scratch_shapes=[
            pltpu.VMEM(grad.shape, grad.dtype),
            pltpu.VMEM(grad.shape, f32),
            pltpu.VMEM(output.shape, output.dtype),
            pltpu.SemaphoreType.DMA((2, 2, COPIES)),
        ],
        compiler_params=pltpu.CompilerParams(vmem_limit_bytes=VMEM_LIMIT),
        name="hand",
    )(grad, output, sums)
    return (output, grad) + tuple(totals)


def per_device(
    n_dp,
    tokens,
    segment_ids,
    cotangent,
    w_query,
    w_key,
    w_value,
    w_output,
    shared_down,
    shared_up,
    w_in,
    w_out,
    gain_one,
    gain_two,
    query_scale,
    query_bias,
    value_scale,
    value_bias,
):
    rows, model = tokens.shape[0] // 2, tokens.shape[1]
    ranks = shared_down.shape[1]
    shards = dict(
        w_query=w_query,
        w_key=w_key,
        w_value=w_value,
        out_t=w_output.T,
        down=shared_down,
        up=shared_up,
        w_in=w_in,
        ff_t=w_out.T,
    )
    stride = n_dp // SLABS
    if stride > 1:
        groups = [list(range(g * stride, (g + 1) * stride)) for g in range(SLABS)]
        gather = functools.partial(lax.all_gather, axis=0, tiled=True, axis_index_groups=groups)
        shards = {n: gather(s, "dp") for n, s in shards.items()}
    arrays = types.SimpleNamespace(
        **shards,
        tokens=tokens,
        cotangent=cotangent,
        segments=segment_ids,
        gain_one=gain_one,
        gain_two=gain_two,
        query_scale=query_scale,
        query_bias=query_bias,
        value_scale=value_scale,
        value_bias=value_bias,
    )
    bits = SLABS.bit_length() - 1
    output, grad, sums, flag = call_layer(stride, bits, n_dp, arrays, rows)
    def halves():
        return call_hand(output, grad, sums)

    def whole():
        core = lax.axis_index("tp")
        own = types.SimpleNamespace(**vars(arrays))
        own.tokens = lax.dynamic_slice_in_dim(tokens, core * rows, rows, 0)
        own.cotangent = lax.dynamic_slice_in_dim(cotangent, core * rows, rows, 0)
        count = segment_ids.shape[0] // 2
        own.segments = lax.dynamic_slice_in_dim(segment_ids, core * count, count, 0)
        half = lax.dynamic_slice_in_dim(arrays.down, core * (ranks // 2), ranks // 2, 1)
        names = ("query", "key", "value", "out_t", "up", "down", "w_in", "ff_t")
        mine = [arrays.w_query, arrays.w_key, arrays.w_value, arrays.out_t, arrays.up, half]
        mine += [arrays.w_in, arrays.ff_t]
        order = tuple(range(bits - 1, -1, -1))
        full = gather_weights(mine, [order] * len(mine), SLABS, stride)
        full = [jnp.concatenate([f[0], f[1]], axis=1) for f in full]
        weights = types.SimpleNamespace(**dict(zip(names, full)))
        for scale, bias, name in (
            (query_scale, query_bias, "query"),
            (value_scale, value_bias, "value"),
        ):
            extra = dot((weights.down * scale).astype(jnp.bfloat16), weights.up) * bias
            setattr(weights, name, (getattr(weights, name) + extra).astype(jnp.bfloat16))
        output, token_grad, parts = whole_sequences(own, weights)
        return call_hand(output, token_grad, call_total(parts, n_dp))

    return lax.cond(flag[0, 0] == 0.0, halves, whole)


def solution(mesh):
    in_specs = (
        P("dp", None),
        P("dp", None),
        P("dp", None),
        P("dp", "tp"),
        P("dp", "tp"),
        P("dp", "tp"),
        P("tp", "dp"),
        P("dp", None),
        P("dp", "tp"),
        P("dp", "tp"),
        P("tp", "dp"),
        P(),
        P(),
        P(),
        P(),
        P(),
        P(),
    )
    out_specs = (P(("dp", "tp"), None), P(("dp", "tp"), None), P(), P(), P(), P())
    return jax.shard_map(
        functools.partial(per_device, mesh.shape["dp"]),
        mesh=mesh,
        in_specs=in_specs,
        out_specs=out_specs,
        check_vma=False,
    )
```
